1024 devices in a mesh: row: 64 (over z_lo, y), col: 16 (over x, z_hi, core).
Axes of the slice: x: 4, y: 4, z: 32 (z_hi: 2, z_lo: 16; z = z_hi * 16 + z_lo), core: 2. Of those that a mesh axis runs over, the one named last changes fastest.
Arguments:
- features: bfloat16 [131072, 256], P('row', 'col'), may hold values from -6 to 6
- tile_values: bfloat16 [64, 192, 128, 128], P('row'), may hold values from -0.15625 to 0.15625
- tile_rows: int32 [64, 192], replicated, may hold values from 0 to 15
- tile_cols: int32 [64, 192], replicated, may hold values from 0 to 1023, as said below
- tile_count: int32 [64], replicated, may hold values from 32 to 192, as said below
- weight: bfloat16 [256, 256], replicated, may hold values from -0.375 to 0.375
- out_bias: float32 [256], replicated, may hold values from -3 to 3
- cotangent: bfloat16 [131072, 256], P('row', 'col'), may hold values from -6 to 6
Outputs:
- activated: bfloat16 [131072, 256], P('row', 'col')
- feature_grad: bfloat16 [131072, 256], P('row', 'col')
- weight_grad: float32 [256, 256], P('col')
- bias_grad: float32 [256], P('col')
The draws below stay inside these ranges and needn't reach their ends.
Inputs may be any that keep to these rules, and one draw needn't show every extreme that they name: tile_cols[g, s] names a tile column of row group g - 1, g or g + 1, counted cyclically over the 64 row groups, where row group h holds tile columns h * 16 to h * 16 + 15. `tile_count`: the live slots of a row group are its first ones; exactly one row group fills all 192 slots in every draw, and every other one has at most 64 live slots.
All inputs are finite; a program needn't handle non-finite values.
Results may differ from the reference program's by a relative error of at most 0.007.
Values may be sent and summed in bfloat16 or wider, within the bound.
A program may use at most 64 MiB of HBM per device.

```python
import math
import jax
import jax.numpy as jnp
import numpy as np
from jax import lax

F = 256
TILE = 128
TR = 16
SLOTS = 192
NT = 1024
NODES = 131072
N_ROW = 64


def draw_tile_cols(key, part):
    key = jax.random.fold_in(key, 11)
    relative = jax.random.randint(key, (N_ROW, SLOTS), 0, 3 * TR)
    groups = (jnp.arange(N_ROW, dtype=jnp.int32)[:, None] - 1 + relative // TR + N_ROW) % N_ROW
    return (groups * TR + relative % TR).astype(jnp.int32)


def draw_tile_count(key, part):
    key = jax.random.fold_in(key, 7)
    first_key, second_key = jax.random.split(key)
    base_counts = jax.random.randint(first_key, (N_ROW,), SLOTS // 6, SLOTS // 3 + 1)
    busiest = jax.random.randint(second_key, (), 0, N_ROW)
    return jnp.where(jnp.arange(N_ROW) == busiest, SLOTS, base_counts).astype(jnp.int32)


def touch_ends(values, stream_key, smallest, top_value):
    spot = [jax.random.randint(jax.random.fold_in(stream_key, axis), (), 0, length) for axis, length in enumerate(values.shape)]
    widest = values.shape.index(max(values.shape))
    next_to = spot[:widest] + [(spot[widest] + 1) % values.shape[widest]] + spot[widest + 1:]
    return values.at[tuple(spot)].set(smallest).at[tuple(next_to)].set(top_value)


def block_levels(own_key, extent, cuts, smallest, high):
    def one(position, parts):
        steps = jax.random.uniform(jax.random.fold_in(jax.random.fold_in(own_key, 6), position), (parts,), jnp.float32, smallest / len(cuts), high / len(cuts))
        return jnp.repeat(jnp.exp(steps), extent[position] // parts).reshape((-1,) + (1,) * (len(extent) - position - 1))

    loudness = one(*cuts[0])
    for cut in cuts[1:]:
        loudness = loudness * one(*cut)
    return loudness


def cumulative_ranks(number_of, skew):
    loads = [(1 << 20) // math.isqrt(grade ** skew) + 1 for grade in range(1, number_of + 1)]
    spread = 1 + sum(loads) // (1 << 30)
    return np.cumsum(np.array([max(1, weight // spread) for weight in loads]))


def ranked_ids(stream_key, shape, count, lean):
    table = cumulative_ranks(count, lean)
    pick = jax.random.randint(jax.random.fold_in(stream_key, 1), shape, 0, int(table[count - 1]))
    grade = jnp.searchsorted(jnp.asarray(table, jnp.int32), pick, side="right")
    return jax.random.permutation(jax.random.fold_in(stream_key, 2), count)[grade].astype(jnp.int32)


def normal_values(stream_key, extent, spread, limit, cuts=(), held_as=jnp.bfloat16):
    values = spread * jax.random.normal(stream_key, extent, jnp.float32)
    if cuts:
        values = values * block_levels(stream_key, extent, cuts, -0.22, 0.18)
    return jnp.clip(values, -limit, limit).astype(held_as)


def setup_inputs(seed: int = 0) -> dict:
    key_list = jax.random.split(jax.random.key(seed), 9)
    features = normal_values(key_list[0], (NODES, F), 1.0, 6.0, ((0, 64), (1, 16)))
    tile_values = normal_values(key_list[1], (N_ROW, SLOTS, TILE, TILE), (12 * TILE) ** -0.5, 0.15625, ((0, 64),))
    tile_rows = touch_ends(ranked_ids(key_list[2], (N_ROW, SLOTS), TR, 2), jax.random.fold_in(key_list[2], 3), 0, TR - 1).astype(jnp.int32)
    tile_cols = draw_tile_cols(jax.random.fold_in(key_list[8], 71), 0)
    tile_count = draw_tile_count(jax.random.fold_in(key_list[8], 71), 0)
    weight = normal_values(key_list[5], (F, F), F ** -0.5, 0.375)
    out_bias = normal_values(key_list[6], (F,), 0.5, 3.0, (), jnp.float32)
    cotangent = normal_values(key_list[7], (NODES, F), 1.0, 6.0, ((0, 64), (1, 16)))
    return dict(features=features, tile_values=tile_values, tile_rows=tile_rows, tile_cols=tile_cols, tile_count=tile_count, weight=weight, out_bias=out_bias, cotangent=cotangent)


def aggregate(tile_values, tile_rows, tile_cols, tile_count, field):
    all_blocks = field.reshape(NT, TILE, F)
    slot_ids = jnp.arange(SLOTS, dtype=jnp.int32)
    row_ids = jnp.arange(TR, dtype=jnp.int32)

    def one_group(packed):
        group_values, group_rows, group_cols, group_count = packed
        live_slots = slot_ids < group_count
        picked = all_blocks[group_cols]
        product = jnp.einsum('sij,sjf->sif', group_values.astype(jnp.float32), picked, precision=lax.Precision.HIGHEST)
        selector = ((group_rows[:, None] == row_ids[None, :]) & live_slots[:, None]).astype(jnp.float32)
        return jnp.einsum('st,sif->tif', selector, product, precision=lax.Precision.HIGHEST)
    result = lax.map(one_group, (tile_values, tile_rows, tile_cols, tile_count))
    return result.reshape(NODES, F)

def reference(features, tile_values, tile_rows, tile_cols, tile_count, weight, out_bias, cotangent):

    def apply_adjacency(field):
        return aggregate(tile_values, tile_rows, tile_cols, tile_count, field)
    aggregated_f, pullback = jax.vjp(apply_adjacency, features.astype(jnp.float32))
    aggregated = aggregated_f.astype(jnp.bfloat16)
    preact = jnp.dot(aggregated, weight, preferred_element_type=jnp.float32) + out_bias
    sigma = jax.nn.sigmoid(preact)
    activated = (preact * sigma).astype(jnp.bfloat16)
    hidden_grad = (cotangent.astype(jnp.float32) * sigma * (1.0 + preact * (1.0 - sigma))).astype(jnp.bfloat16)
    scale_factor = 1.0 / jnp.sqrt(jnp.float32(NODES))
    weight_grad = jnp.dot(aggregated.T, hidden_grad, preferred_element_type=jnp.float32) * scale_factor
    bias_grad = lax.optimization_barrier(jnp.sum(hidden_grad.astype(jnp.float32), axis=0)) * scale_factor
    aggregated_grad = jnp.dot(hidden_grad, weight.T, preferred_element_type=jnp.float32).astype(jnp.bfloat16)
    feature_grad = pullback(aggregated_grad.astype(jnp.float32))[0].astype(jnp.bfloat16)
    return (activated, feature_grad, weight_grad, bias_grad)
```

```python
import functools
import math

import jax
import jax.numpy as jnp
from jax import lax
from jax.experimental import pallas as pl
from jax.experimental.pallas import tpu as pltpu
from jax.sharding import PartitionSpec as P

MESH = pl.DeviceIdType.MESH
F32 = jnp.float32
BF16 = jnp.bfloat16
T = 128
TR = 16
W = 16
ROWS = 64
COLS = 16
UNROLL = 8
CHUNKS = 4
NT = (((1,), (1,)), ((), ()))
NN = (((1,), (0,)), ((), ()))


def dot(a, b, dims=NN):
    return lax.dot_general(a, b, dims, preferred_element_type=F32)


def select_sum(onehot, prods, targets, out):
    slots = onehot.shape[1]
    for f in range(W):
        v = prods[pl.ds(f, slots, stride=W), :]
        hi = v.astype(BF16)
        lo = (v - hi.astype(F32)).astype(BF16)
        out[pl.ds(f, targets, stride=W), :] = dot(onehot, hi) + dot(onehot, lo)


def kernel(
    slots,
    scale,
    ft,
    ct,
    tv,
    rows_h,
    cols_h,
    count_h,
    w_h,
    bias_h,
    act_o,
    fg_o,
    wg_o,
    bg_o,
    rows_s,
    cols_s,
    count_s,
    rows_v,
    cols_v,
    w,
    bias,
    win,
    cols3,
    tvv,
    prods,
    sums,
    wt,
    cot_buf,
    agg_send,
    agg_buf,
    ag_send,
    ag_buf,
    act_send,
    act_buf,
    halo_send,
    halo_buf,
    s1_send,
    s1_buf,
    r1_send,
    r1_buf,
    r2_send,
    r2_buf,
    r3_send,
    r3_buf,
    y_send,
    y_buf,
    tile_sem,
    own_sem,
    halo_ss,
    halo_rs,
    back_ss,
    back_rs,
    ss,
    rs,
):
    g = lax.axis_index("row")
    me = lax.axis_index("col")
    z_lo, y = g // 4, g % 4
    za, zb = z_lo // 4, z_lo % 4
    x, zh, core = me // 4, (me // 2) % 2, me % 2
    prev, nxt = (g + ROWS - 1) % ROWS, (g + 1) % ROWS

    col_peers = []
    for dz in (1, 0):
        for dx in (2, 1, 3, 0):
            for dc in (0, 1):
                if (dz, dx, dc) != (0, 0, 0):
                    col_peers.append(((x + dx) % 4) * 4 + ((zh + dz) % 2) * 2 + (core + dc) % 2)
    z_peers = []
    for dx in (2, 1, 3, 0):
        for dy in (2, 1, 3, 0):
            for dc in (0, 1):
                if (dx, dy, dc) != (0, 0, 0):
                    px, py, pc = (x + dx) % 4, (y + dy) % 4, (core + dc) % 2
                    part = 2 * (4 * px + 2 * (py // 2) + pc) + py % 2
                    z_peers.append((z_lo * 4 + py, px * 4 + zh * 2 + pc, part))
    my_part = 2 * (4 * x + 2 * (y // 2) + core) + y % 2
    my_rank = x * 8 + y * 2 + core
    b_peers = [((za * 4 + (zb + d) % 4) * 4 + y, me) for d in (1, 2, 3)]
    a_peers = [((((za + d) % 4) * 4 + zb) * 4 + y, me) for d in (1, 2, 3)]
    h_peers = [(g, x * 4 + ((zh + 1) % 2) * 2 + core)]
    y_peers = [(z_lo * 4 + (y + d) % 4, me) for d in (1, 2, 3)]

    step = slots // CHUNKS
    tile_copies = [
        pltpu.make_async_copy(
            tv.at[0, pl.ds(k * step, step)], tvv.at[pl.ds(k * step, step)], tile_sem.at[k]
        )
        for k in range(CHUNKS)
    ]
    own_ft = pltpu.make_async_copy(ft, win.at[1], own_sem.at[0])
    own_ct = pltpu.make_async_copy(
        ct.at[:, pl.ds(pl.multiple_of(me * T, T), T)], cot_buf.at[me], own_sem.at[1]
    )
    index_copies = [
        pltpu.make_async_copy(src, dst, own_sem.at[2 + k])
        for k, (src, dst) in enumerate(
            (
                (cols_h, cols_s),
                (rows_h, rows_v),
                (cols_h, cols_v),
                (count_h, count_s),
                (w_h, w),
                (bias_h, bias),
                (rows_h, rows_s),
            )
        )
    ]
    for copy in index_copies:
        copy.start()
    own_ft.start()
    own_ct.start()
    for copy in tile_copies:
        copy.start()

    barrier = pltpu.get_barrier_semaphore()
    everyone = (
        [(prev, me), (nxt, me)]
        + [(g, c) for c in col_peers]
        + [(r, c) for r, c, _ in z_peers]
        + b_peers
        + a_peers
        + h_peers
        + y_peers
    )
    for peer in everyone:
        pl.semaphore_signal(barrier, inc=1, device_id=peer, device_id_type=MESH)
    pl.semaphore_wait(barrier, len(everyone))

    def send(src, dst, send_sem, recv_sem, peer):
        copy = pltpu.make_async_remote_copy(
            src_ref=src,
            dst_ref=dst,
            send_sem=send_sem,
            recv_sem=recv_sem,
            device_id=peer,
            device_id_type=MESH,
        )
        copy.start()
        return copy

    def await_blocks(buf, count, sem):
        view = buf.at[pl.ds(0, count)]
        pltpu.make_async_copy(view, view, sem).wait()

    to_prev = send(ft, win.at[2], halo_ss.at[0], halo_rs.at[0], (prev, me))
    to_next = send(ft, win.at[0], halo_ss.at[1], halo_rs.at[1], (nxt, me))
    for c in col_peers:
        send(
            ct.at[:, pl.ds(pl.multiple_of(c * T, T), T)],
            cot_buf.at[me],
            ss.at[0],
            rs.at[0],
            (g, c),
        )

    for copy in index_copies:
        copy.wait()
    count = count_s[g]
    live = lax.broadcasted_iota(jnp.int32, (TR, slots), 1) < count
    row_ids = lax.broadcasted_iota(jnp.int32, (TR, slots), 0)
    by_row = jnp.where((rows_v[pl.ds(g, 1), :] == row_ids) & live, 1.0, 0.0).astype(BF16)
    own_cols = cols_v[pl.ds(g, 1), :]
    rel = ((lax.div(own_cols, TR) - g + (ROWS + 1)) % ROWS) * TR + lax.rem(own_cols, TR)
    by_col = [
        jnp.where((rel == row_ids + k * TR) & live, 1.0, 0.0).astype(BF16) for k in range(3)
    ]
    wt[...] = w[...].T
    bias_t = jnp.broadcast_to(bias[...], (T, W * COLS)).T

    own_ft.wait()
    to_prev.wait_recv()
    to_next.wait_recv()

    for k in range(3):
        for b in range(TR):
            cols3[k * TR + b] = win[k, :, b * T : (b + 1) * T]

    def forward(i, _):
        for u in range(UNROLL):
            s = i * UNROLL + u
            col = cols_s[g, s]
            grp = jnp.minimum(lax.rem(lax.div(col, TR) - g + (ROWS + 1), ROWS), 2)
            p = dot(cols3[grp * TR + lax.rem(col, TR)], tvv[s], NT)
            prods[pl.ds(pl.multiple_of(s * W, W), W), :] = p
        return 0

    for k in range(CHUNKS):
        tile_copies[k].wait()
        lax.fori_loop(k * step // UNROLL, (k + 1) * step // UNROLL, forward, 0)
    select_sum(by_row, prods, TR, sums)
    agg_send[...] = sums[0 : TR * W, :].astype(BF16).reshape(TR, W, T)
    for c in col_peers:
        send(agg_send.at[c], agg_buf.at[me], ss.at[1], rs.at[1], (g, c))
    agg_buf[pl.ds(me, 1)] = agg_send[pl.ds(me, 1)]
    await_blocks(cot_buf, COLS - 1, rs.at[0])
    own_ct.wait()
    await_blocks(agg_buf, COLS - 1, rs.at[1])

    agg_t = agg_buf[...].reshape(COLS * W, T)
    pre = dot(wt[...], agg_t) + bias_t
    sigma = jax.nn.sigmoid(pre)
    cot = cot_buf[...].reshape(COLS * W, T).astype(F32)
    hg = (cot * sigma * (1.0 + pre * (1.0 - sigma))).astype(BF16)
    ag_send[...] = dot(w[...], hg).astype(BF16).reshape(COLS, W, T)
    for c in col_peers:
        send(ag_send.at[c], ag_buf.at[me], ss.at[2], rs.at[2], (g, c))
    ag_buf[pl.ds(me, 1)] = ag_send[pl.ds(me, 1)]
    act_send[...] = (pre * sigma).astype(BF16).reshape(COLS, W, T)
    for c in col_peers:
        send(act_send.at[c], act_buf.at[me], ss.at[3], rs.at[3], (g, c))
    act_buf[pl.ds(me, 1)] = act_send[pl.ds(me, 1)]

    s1_send[:, :, 0 : COLS * W] = dot(agg_t, hg, NT).reshape(32, 8, COLS * W)
    bias_rows = dot(jnp.ones((8, T), BF16), hg, NT)
    bias_tile = jnp.where(
        lax.broadcasted_iota(jnp.int32, (8, 128), 0) < 4, bias_rows[:, 0:128], bias_rows[:, 128:256]
    )
    s1_send[:, :, COLS * W :] = jnp.broadcast_to(bias_tile[None], (32, 8, 128))
    for r, c, part in z_peers:
        send(s1_send.at[part], s1_buf.at[my_rank], ss.at[4], rs.at[4], (r, c))
    s1_buf[pl.ds(my_rank, 1)] = s1_send[pl.ds(my_part, 1)]

    def exchange(value, send_buf, buf, mine, peers, n):
        send_buf[...] = value
        for peer in peers:
            send(send_buf, buf.at[mine], ss.at[n], rs.at[n], peer)
        buf[pl.ds(mine, 1)] = value[None]

    def total(buf, count, n):
        await_blocks(buf, count - 1, rs.at[n])
        return jnp.sum(buf[...], axis=0)

    exchange(total(s1_buf, 32, 4), r1_send, r1_buf, zb, b_peers, 5)

    def backward(i, _):
        for u in range(UNROLL):
            s = i * UNROLL + u
            p = dot(ag_buf[rows_s[g, s]], tvv[s])
            prods[pl.ds(pl.multiple_of(s * W, W), W), :] = p
        return 0

    await_blocks(ag_buf, COLS - 1, rs.at[2])
    lax.fori_loop(0, slots // UNROLL // 2, backward, 0)
    exchange(total(r1_buf, 4, 5), r2_send, r2_buf, za, a_peers, 6)
    lax.fori_loop(slots // UNROLL // 2, slots // UNROLL, backward, 0)
    back = []
    for k, peer in ((0, prev), (2, nxt)):
        select_sum(by_col[k], prods, TR, sums)
        halo_send[k // 2] = sums[0 : TR * W, :].astype(BF16).reshape(TR, W, T)
        back.append(
            send(
                halo_send.at[k // 2],
                halo_buf.at[k // 2],
                back_ss.at[k // 2],
                back_rs.at[k // 2],
                (peer, me),
            )
        )
    select_sum(by_col[1], prods, TR, sums)
    exchange(total(r2_buf, 4, 6), r3_send, r3_buf, zh, h_peers, 7)

    await_blocks(act_buf, COLS - 1, rs.at[3])
    for k in range(COLS):
        act_o[:, k * T : (k + 1) * T] = act_buf[k]
    for copy in back:
        copy.wait_recv()
    for k in range(COLS):
        fg_o[:, k * T : (k + 1) * T] = (
            sums[k * W : (k + 1) * W, :] + halo_buf[0, k].astype(F32) + halo_buf[1, k].astype(F32)
        ).astype(BF16)
    exchange(total(r3_buf, 2, 7), y_send, y_buf, y, y_peers, 8)
    await_blocks(y_buf, 3, rs.at[8])
    wg_o[0:8, :] = y_buf[2 * zh, :, 0 : COLS * W] * scale
    wg_o[8:16, :] = y_buf[2 * zh + 1, :, 0 : COLS * W] * scale
    tile = y_buf[y, :, COLS * W :]
    row = jnp.where(me < 8, tile[0:1, :], tile[4:5, :]) * scale
    bg_o[...] = pltpu.roll(row, (128 - (me % 8) * W) % 128, 1)[:, 0:W]

    to_prev.wait_send()
    to_next.wait_send()
    for copy in back:
        copy.wait_send()
    for n, buf in ((0, cot_buf), (1, agg_buf), (2, ag_buf), (3, act_buf)):
        await_blocks(buf, COLS - 1, ss.at[n])
    await_blocks(s1_buf, 31, ss.at[4])
    await_blocks(r1_buf, 3, ss.at[5])
    await_blocks(r2_buf, 3, ss.at[6])
    await_blocks(r3_buf, 1, ss.at[7])
    await_blocks(y_buf, 3, ss.at[8])


def on_device(features, tile_values, tile_rows, tile_cols, tile_count, weight, out_bias, cotangent):
    slots = tile_values.shape[1]
    nodes = features.shape[0]
    width = weight.shape[0]
    scale = 1.0 / math.sqrt(nodes * ROWS)
    vmem = pl.BlockSpec(memory_space=pltpu.VMEM)
    hbm = pl.BlockSpec(memory_space=pltpu.HBM)
    blocks = pltpu.VMEM((COLS, W, T), BF16)
    parts = lambda n: pltpu.VMEM((n, 8, width + 128), F32)
    part = pltpu.VMEM((8, width + 128), F32)
    act, fg, wg, bg = pl.pallas_call(
        functools.partial(kernel, slots, scale),
        out_shape=(
            jax.ShapeDtypeStruct((W, nodes), BF16),
            jax.ShapeDtypeStruct((W, nodes), BF16),
            jax.ShapeDtypeStruct((W, width), F32),
            jax.ShapeDtypeStruct((1, W), F32),
        ),
        in_specs=[hbm] * 8,
        out_specs=(vmem,) * 4,
        scratch_shapes=[
            pltpu.SMEM(tile_rows.shape, jnp.int32),
            pltpu.SMEM(tile_cols.shape, jnp.int32),
            pltpu.SMEM(tile_count.shape, jnp.int32),
            pltpu.VMEM(tile_rows.shape, jnp.int32),
            pltpu.VMEM(tile_cols.shape, jnp.int32),
            pltpu.VMEM(weight.shape, BF16),
            pltpu.VMEM((1, width), F32),
            pltpu.VMEM((3, W, nodes), BF16),
            pltpu.VMEM((3 * TR, W, T), BF16),
            pltpu.VMEM((slots, T, T), BF16),
            pltpu.VMEM((slots * W, T), F32),
            pltpu.VMEM((TR * W, T), F32),
            pltpu.VMEM((width, width), BF16),
            blocks,
            blocks,
            blocks,
            blocks,
            blocks,
            blocks,
            blocks,
            pltpu.VMEM((2, TR, W, T), BF16),
            pltpu.VMEM((2, TR, W, T), BF16),
            parts(32),
            parts(32),
            part,
            parts(4),
            part,
            parts(4),
            part,
            parts(2),
            part,
            parts(4),
            pltpu.SemaphoreType.DMA((CHUNKS,)),
            pltpu.SemaphoreType.DMA((9,)),
            pltpu.SemaphoreType.DMA((2,)),
            pltpu.SemaphoreType.DMA((2,)),
            pltpu.SemaphoreType.DMA((2,)),
            pltpu.SemaphoreType.DMA((2,)),
            pltpu.SemaphoreType.DMA((9,)),
            pltpu.SemaphoreType.DMA((9,)),
        ],
        compiler_params=pltpu.CompilerParams(
            collective_id=0, has_side_effects=True, vmem_limit_bytes=56 * 1024 * 1024
        ),
        name="graph_layer",
    )(
        features.T,
        cotangent.T,
        tile_values,
        tile_rows,
        tile_cols,
        tile_count,
        weight,
        out_bias.reshape(1, width),
    )
    return act.T, fg.T, wg, bg.reshape(W)


def solution(mesh):
    in_specs = (
        P("row", "col"),
        P("row", None, None, None),
        P(),
        P(),
        P(),
        P(),
        P(),
        P("row", "col"),
    )
    out_specs = (P("row", "col"), P("row", "col"), P("col", None), P("col"))
    return jax.shard_map(
        on_device, mesh=mesh, in_specs=in_specs, out_specs=out_specs, check_vma=False
    )
```

```python
import functools
import math

import jax
import jax.numpy as jnp
from jax import lax
from jax.experimental import pallas as pl
from jax.experimental.pallas import tpu as pltpu
from jax.sharding import PartitionSpec as P

MESH = pl.DeviceIdType.MESH
F32 = jnp.float32
BF16 = jnp.bfloat16
T = 128
TR = 16
W = 16
W2 = 2 * W
ROWS = 64
COLS = 16
UNROLL = 16
CHUNKS = 4
NT = (((1,), (1,)), ((), ()))
NN = (((1,), (0,)), ((), ()))


def dot(a, b, dims=NN):
    return lax.dot_general(a, b, dims, preferred_element_type=F32)


def select_sum(onehot, prods, stride, first, count, targets, out):
    slots = onehot.shape[1]
    for f in range(count):
        v = prods[pl.ds(first + f, slots, stride=stride), :]
        hi = v.astype(BF16)
        lo = (v - hi.astype(F32)).astype(BF16)
        out[pl.ds(f, targets, stride=count), :] = dot(onehot, hi) + dot(onehot, lo)


def kernel(
    slots,
    scale,
    ft,
    ct,
    tv,
    rows_h,
    cols_h,
    count_h,
    w_h,
    bias_h,
    act_o,
    fg_o,
    wg_o,
    bg_o,
    rows_s,
    cols_s,
    count_s,
    rows_v,
    cols_v,
    w,
    bias,
    win,
    cols3,
    tvv,
    prods,
    sums,
    wt,
    bias_t,
    cot_far,
    cot_buf,
    agg_send,
    agg_buf,
    ag_send,
    ag_buf,
    act_full,
    act_buf,
    halo_send,
    halo_buf,
    s1_send,
    s1_buf,
    r1_send,
    r1_buf,
    r2_send,
    r2_buf,
    y_send,
    y_buf,
    tile_sem,
    own_sem,
    halo_ss,
    halo_rs,
    far_ss,
    far_rs,
    back_ss,
    back_rs,
    ss,
    rs,
):
    g = lax.axis_index("row")
    me = lax.axis_index("col")
    z_lo, y = g // 4, g % 4
    za, zb = z_lo // 4, z_lo % 4
    x, zh, core = me // 4, (me // 2) % 2, me % 2
    n = x * 2 + core
    other = (zh + 1) % 2
    mate = x * 4 + other * 2 + core
    z_prev, z_next = (zh + (ROWS - g) // ROWS) % 2, (zh + (g + 1) // ROWS) % 2
    prev = ((g + ROWS - 1) % ROWS, x * 4 + z_prev * 2 + core)
    nxt = ((g + 1) % ROWS, x * 4 + z_next * 2 + core)

    near = []
    plane = []
    for dx in (2, 1, 3, 0):
        for dy in (2, 1, 3, 0):
            for dc in (0, 1):
                px, py, pc = (x + dx) % 4, (y + dy) % 4, (core + dc) % 2
                if (dx, dy, dc) != (0, 0, 0):
                    device = (z_lo * 4 + py, px * 4 + zh * 2 + pc)
                    plane.append((device, (px * 2 + pc) * 4 + py))
                    if dy == 0:
                        near.append((device, px * 2 + pc))
    b_peers = [((za * 4 + (zb + d) % 4) * 4 + y, me) for d in (1, 2, 3)]
    a_peers = [((((za + d) % 4) * 4 + zb) * 4 + y, me) for d in (2, 1, 3)]
    y_peers = [(z_lo * 4 + (y + d) % 4, me) for d in (1, 2, 3)]

    def wide(k):
        return pl.ds(pl.multiple_of(k * 2 * T, 2 * T), 2 * T)

    barrier = pltpu.get_barrier_semaphore()
    everyone = [(g, mate), prev, nxt] + a_peers + b_peers + [device for device, _ in plane]
    for peer in everyone:
        pl.semaphore_signal(barrier, inc=1, device_id=peer, device_id_type=MESH)

    step = slots // CHUNKS
    local = [
        pltpu.make_async_copy(src, dst, own_sem.at[k])
        for k, (src, dst) in enumerate(
            (
                (ft, win.at[zh, 1]),
                (ct.at[:, wide(n)], cot_buf.at[me]),
                (cols_h, cols_s),
                (rows_h, rows_s),
                (cols_h, cols_v),
                (rows_h, rows_v),
                (count_h, count_s),
                (w_h, w),
                (bias_h, bias),
            )
        )
    ] + [
        pltpu.make_async_copy(
            tv.at[0, pl.ds(k * step, step)], tvv.at[pl.ds(k * step, step)], tile_sem.at[k]
        )
        for k in range(CHUNKS)
    ]
    for copy in local:
        copy.start()
    for copy in local:
        copy.wait()

    count = count_s[g]
    live = lax.broadcasted_iota(jnp.int32, (TR, slots), 1) < count
    row_ids = lax.broadcasted_iota(jnp.int32, (TR, slots), 0)
    by_row = jnp.where((rows_v[pl.ds(g, 1), :] == row_ids) & live, 1.0, 0.0).astype(BF16)
    own_cols = cols_v[pl.ds(g, 1), :]
    rel = ((lax.div(own_cols, TR) - g + (ROWS + 1)) % ROWS) * TR + lax.rem(own_cols, TR)
    by_col = [
        jnp.where((rel == row_ids + k * TR) & live, 1.0, 0.0).astype(BF16) for k in range(3)
    ]
    wt[...] = w[...].T
    bias_t[...] = jnp.broadcast_to(bias[...], (2 * T, W * COLS)).T

    pl.semaphore_wait(barrier, len(everyone))

    def send(src, dst, send_sem, recv_sem, peer):
        copy = pltpu.make_async_remote_copy(
            src_ref=src,
            dst_ref=dst,
            send_sem=send_sem,
            recv_sem=recv_sem,
            device_id=peer,
            device_id_type=MESH,
        )
        copy.start()
        return copy

    def await_bytes(view, sem):
        pltpu.make_async_copy(view, view, sem).wait()

    far_ft = send(ft, win.at[zh, 1], far_ss.at[0], far_rs.at[0], (g, mate))
    far_ct = send(ct, cot_far, far_ss.at[1], far_rs.at[1], (g, mate))

    def to_sides(src, half):
        send(src, win.at[half, 0], halo_ss.at[half], halo_rs.at[half], nxt)
        send(src, win.at[half, 2], halo_ss.at[2 + half], halo_rs.at[2 + half], prev)

    to_sides(ft, zh)
    for device, k in near:
        send(ct.at[:, wide(k)], cot_buf.at[me], ss.at[0], rs.at[0], device)
    far_ft.wait_recv()
    to_sides(win.at[other, 1], other)
    far_ct.wait_recv()
    own_cot = pltpu.make_async_copy(cot_far.at[:, wide(n)], cot_buf.at[mate], own_sem.at[1])
    own_cot.start()
    for device, k in near:
        send(cot_far.at[:, wide(k)], cot_buf.at[mate], ss.at[1], rs.at[1], device)

    for k in range(4):
        await_bytes(win.at[0, 0], halo_rs.at[k])
    for h in range(2):
        for k in range(3):
            for b in range(TR):
                cols3[k * TR + b, h * W : (h + 1) * W] = win[h, k, :, b * T : (b + 1) * T]

    def forward(i, _):
        for u in range(UNROLL):
            s = i * UNROLL + u
            col = cols_s[g, s]
            grp = jnp.minimum(lax.rem(lax.div(col, TR) - g + (ROWS + 1), ROWS), 2)
            p = dot(cols3[grp * TR + lax.rem(col, TR)], tvv[s], NT)
            prods[pl.ds(pl.multiple_of(s * W2, W2), W2), :] = p
        return 0

    lax.fori_loop(0, slots // UNROLL, forward, 0)
    select_sum(by_row, prods, W2, 0, W2, TR, sums)
    for r in range(TR):
        for h in range(2):
            first = r * W2 + h * W
            agg_send[r // 2, h, r % 2] = sums[first : first + W, :].astype(BF16)
    for device, k in near:
        send(agg_send.at[k], agg_buf.at[x, :, core], ss.at[2], rs.at[2], device)
    own_agg = pltpu.make_async_copy(agg_send.at[n], agg_buf.at[x, :, core], own_sem.at[2])
    own_agg.start()
    await_bytes(cot_buf.at[pl.ds(0, 7)], rs.at[0])
    await_bytes(cot_buf.at[pl.ds(0, 7)], rs.at[1])
    own_cot.wait()
    own_agg.wait()
    await_bytes(agg_send.at[pl.ds(0, 7)], rs.at[2])

    agg_t = jnp.concatenate(
        [agg_buf[:, :, :, t].reshape(COLS * W, T) for t in range(2)], axis=1
    )
    pre = dot(wt[...], agg_t) + bias_t[...]
    sigma = jax.nn.sigmoid(pre)
    cot = cot_buf[...].reshape(COLS * W, 2 * T).astype(F32)
    hg = (cot * sigma * (1.0 + pre * (1.0 - sigma))).astype(BF16)
    ag = dot(w[...], hg).astype(BF16)
    for k in range(8):
        for h in range(2):
            first = ((k // 2) * 4 + h * 2 + k % 2) * W
            for t in range(2):
                ag_send[k, t, h] = ag[first : first + W, t * T : (t + 1) * T]
    for device, k in near:
        send(ag_send.at[k], ag_buf.at[pl.ds(2 * n, 2)], ss.at[3], rs.at[3], device)
    own_ag = pltpu.make_async_copy(ag_send.at[n], ag_buf.at[pl.ds(2 * n, 2)], own_sem.at[3])
    own_ag.start()

    agg_half = jnp.concatenate(
        [agg_buf[:, pl.ds(zh, 1), :, t].reshape(COLS * W // 2, T) for t in range(2)], axis=1
    )
    wg = dot(agg_half, hg, NT)
    for k in range(8):
        for j in range(4):
            first = k * W + (j // 2) * 8
            s1_send[k * 4 + j, 0] = wg[first : first + 8, (j % 2) * T : (j % 2 + 1) * T]
    bias_rows = dot(jnp.ones((8, 2 * T), BF16), hg, NT)
    bias_tile = jnp.where(
        lax.broadcasted_iota(jnp.int32, (8, 128), 0) < 4, bias_rows[:, 0:128], bias_rows[:, 128:256]
    )
    for k in range(32):
        s1_send[k, 1] = bias_tile
    for device, k in plane:
        send(s1_send.at[k], s1_buf.at[n * 4 + y], ss.at[5], rs.at[5], device)
    s1_buf[pl.ds(n * 4 + y, 1)] = s1_send[pl.ds(n * 4 + y, 1)]
    act_full[...] = (pre * sigma).astype(BF16).reshape(COLS, W, 2 * T)
    for device, k in near:
        send(act_full.at[device[1]], act_buf.at[n], ss.at[4], rs.at[4], device)
    act_buf[pl.ds(n, 1)] = act_full[pl.ds(me, 1)]

    def exchange(value, send_buf, buf, mine, peers, k):
        send_buf[...] = value
        for peer in peers:
            send(send_buf, buf.at[mine], ss.at[k], rs.at[k], peer)
        buf[pl.ds(mine, 1)] = value[None]

    def total(buf, others, k):
        await_bytes(buf.at[pl.ds(0, others)], rs.at[k])
        return jnp.sum(buf[...], axis=0)

    def backward(i, _):
        for u in range(UNROLL):
            s = i * UNROLL + u
            p = dot(ag_buf[rows_s[g, s]].reshape(W2, T), tvv[s])
            prods[pl.ds(pl.multiple_of(s * W2, W2), W2), :] = p
        return 0

    await_bytes(ag_send.at[pl.ds(0, 7)], rs.at[3])
    own_ag.wait()
    turns = slots // UNROLL
    lax.fori_loop(0, turns // 3, backward, 0)
    exchange(total(s1_buf, 31, 5), r1_send, r1_buf, zb, b_peers, 6)
    lax.fori_loop(turns // 3, turns, backward, 0)
    exchange(total(r1_buf, 3, 6), r2_send, r2_buf, za, a_peers, 7)
    back = []
    for k, (peer, half) in enumerate(((prev, z_prev), (nxt, z_next))):
        select_sum(by_col[2 * k], prods, W2, half * W, W, TR, sums)
        halo_send[k] = sums[0 : TR * W, :].astype(BF16).reshape(TR, W, T)
        back.append(send(halo_send.at[k], halo_buf.at[k], back_ss.at[k], back_rs.at[k], peer))
    select_sum(by_col[1], prods, W2, zh * W, W, TR, sums)

    await_bytes(act_buf.at[pl.ds(0, 7)], rs.at[4])
    for k in range(8):
        act_o[:, k * 2 * T : (k + 1) * 2 * T] = act_buf[k]
    for copy in back:
        copy.wait_recv()
    for k in range(TR):
        fg_o[:, k * T : (k + 1) * T] = (
            sums[k * W : (k + 1) * W, :] + halo_buf[0, k].astype(F32) + halo_buf[1, k].astype(F32)
        ).astype(BF16)
    exchange(total(r2_buf, 3, 7), y_send, y_buf, y, y_peers, 8)

    far_ft.wait_send()
    far_ct.wait_send()
    for k in range(4):
        await_bytes(win.at[0, 0], halo_ss.at[k])
    for copy in back:
        copy.wait_send()
    for k, view in (
        (0, cot_buf.at[pl.ds(0, 7)]),
        (1, cot_buf.at[pl.ds(0, 7)]),
        (2, agg_send.at[pl.ds(0, 7)]),
        (3, ag_send.at[pl.ds(0, 7)]),
        (4, act_buf.at[pl.ds(0, 7)]),
        (5, s1_buf.at[pl.ds(0, 31)]),
        (6, r1_buf.at[pl.ds(0, 3)]),
        (7, r2_buf.at[pl.ds(0, 3)]),
        (8, y_buf.at[pl.ds(0, 3)]),
    ):
        await_bytes(view, ss.at[k])
    await_bytes(y_buf.at[pl.ds(0, 3)], rs.at[8])
    for j in range(4):
        wg_o[(j // 2) * 8 : (j // 2 + 1) * 8, (j % 2) * T : (j % 2 + 1) * T] = y_buf[j, 0] * scale
    row = jnp.where(me < 8, y_buf[0, 1, 0:1], y_buf[0, 1, 4:5]) * scale
    bg_o[...] = pltpu.roll(row, (128 - (me % 8) * W) % 128, 1)[:, 0:W]


def on_device(features, tile_values, tile_rows, tile_cols, tile_count, weight, out_bias, cotangent):
    slots = tile_values.shape[1]
    nodes = features.shape[0]
    width = weight.shape[0]
    scale = 1.0 / math.sqrt(nodes * ROWS)
    vmem = pl.BlockSpec(memory_space=pltpu.VMEM)
    hbm = pl.BlockSpec(memory_space=pltpu.HBM)
    parts = lambda k: pltpu.VMEM((k, 2, 8, T), F32)
    part = pltpu.VMEM((2, 8, T), F32)
    act, fg, wg, bg = pl.pallas_call(
        functools.partial(kernel, slots, scale),
        out_shape=(
            jax.ShapeDtypeStruct((W, nodes), BF16),
            jax.ShapeDtypeStruct((W, nodes), BF16),
            jax.ShapeDtypeStruct((W, width), F32),
            jax.ShapeDtypeStruct((1, W), F32),
        ),
        in_specs=[hbm] * 8,
        out_specs=(vmem,) * 4,
        scratch_shapes=[
            pltpu.SMEM(tile_rows.shape, jnp.int32),
            pltpu.SMEM(tile_cols.shape, jnp.int32),
            pltpu.SMEM(tile_count.shape, jnp.int32),
            pltpu.VMEM(tile_rows.shape, jnp.int32),
            pltpu.VMEM(tile_cols.shape, jnp.int32),
            pltpu.VMEM(weight.shape, BF16),
            pltpu.VMEM((1, width), F32),
            pltpu.VMEM((2, 3, W, nodes), BF16),
            pltpu.VMEM((3 * TR, W2, T), BF16),
            pltpu.VMEM((slots, T, T), BF16),
            pltpu.VMEM((slots * W2, T), F32),
            pltpu.VMEM((TR * W2, T), F32),
            pltpu.VMEM((width, width), BF16),
            pltpu.VMEM((width, 2 * T), F32),
            pltpu.VMEM((W, nodes), BF16),
            pltpu.VMEM((COLS, W, 2 * T), BF16),
            pltpu.VMEM((8, 2, 2, W, T), BF16),
            pltpu.VMEM((4, 2, 2, 2, W, T), BF16),
            pltpu.VMEM((8, 2, 2, W, T), BF16),
            pltpu.VMEM((TR, 2, W, T), BF16),
            pltpu.VMEM((COLS, W, 2 * T), BF16),
            pltpu.VMEM((8, W, 2 * T), BF16),
            pltpu.VMEM((2, TR, W, T), BF16),
            pltpu.VMEM((2, TR, W, T), BF16),
            parts(32),
            parts(32),
            part,
            parts(4),
            part,
            parts(4),
            part,
            parts(4),
            pltpu.SemaphoreType.DMA((CHUNKS,)),
            pltpu.SemaphoreType.DMA((9,)),
            pltpu.SemaphoreType.DMA((4,)),
            pltpu.SemaphoreType.DMA((4,)),
            pltpu.SemaphoreType.DMA((2,)),
            pltpu.SemaphoreType.DMA((2,)),
            pltpu.SemaphoreType.DMA((2,)),
            pltpu.SemaphoreType.DMA((2,)),
            pltpu.SemaphoreType.DMA((9,)),
            pltpu.SemaphoreType.DMA((9,)),
        ],
        compiler_params=pltpu.CompilerParams(
            collective_id=0, has_side_effects=True, vmem_limit_bytes=32 * 1024 * 1024
        ),
        name="graph_layer",
    )(
        features.T,
        cotangent.T,
        tile_values,
        tile_rows,
        tile_cols,
        tile_count,
        weight,
        out_bias.reshape(1, width),
    )
    return act.T, fg.T, wg, bg.reshape(W)


def solution(mesh):
    in_specs = (
        P("row", "col"),
        P("row", None, None, None),
        P(),
        P(),
        P(),
        P(),
        P(),
        P("row", "col"),
    )
    out_specs = (P("row", "col"), P("row", "col"), P("col", None), P("col"))
    return jax.shard_map(
        on_device, mesh=mesh, in_specs=in_specs, out_specs=out_specs, check_vma=False
    )
```

```python
import functools
import math

import jax
import jax.numpy as jnp
from jax import lax
from jax.experimental import pallas as pl
from jax.experimental.pallas import tpu as pltpu
from jax.sharding import PartitionSpec as P

MESH = pl.DeviceIdType.MESH
F32 = jnp.float32
BF16 = jnp.bfloat16
T = 128
TR = 16
W = 16
W2 = 2 * W
ROWS = 64
COLS = 16
UNROLL = 48
CHUNKS = 4
NT = (((1,), (1,)), ((), ()))
NN = (((1,), (0,)), ((), ()))


def dot(a, b, dims=NN):
    return lax.dot_general(a, b, dims, preferred_element_type=F32)


def select_sum(onehot, prods, stride, first, count, targets, out):
    slots = onehot.shape[1]
    for f in range(count):
        v = prods[pl.ds(first + f, slots, stride=stride), :]
        out[pl.ds(f, targets, stride=count), :] = dot(onehot, v.astype(BF16))


def kernel(
    slots,
    scale,
    ft,
    ct,
    tv,
    rows_h,
    cols_h,
    count_h,
    w_h,
    bias_h,
    act_o,
    fg_o,
    wg_o,
    bg_o,
    rows_s,
    cols_s,
    count_s,
    rows_v,
    cols_v,
    w,
    bias,
    win,
    cols3,
    tvv,
    tvt,
    prods,
    sums,
    wt,
    bias_t,
    cot_far,
    cot_buf,
    agg_send,
    agg_buf,
    ag_send,
    ag_buf,
    act_full,
    act_buf,
    halo_send,
    halo_buf,
    s1_send,
    s1_buf,
    r1_send,
    r1_buf,
    r2_send,
    r2_buf,
    y_send,
    y_buf,
    tile_sem,
    own_sem,
    halo_ss,
    halo_rs,
    far_ss,
    far_rs,
    back_ss,
    back_rs,
    ss,
    rs,
):
    g = lax.axis_index("row")
    me = lax.axis_index("col")
    z_lo, y = g // 4, g % 4
    x, zh, core = me // 4, (me // 2) % 2, me % 2
    n = x * 2 + core
    other = (zh + 1) % 2
    mate = x * 4 + other * 2 + core
    z_prev, z_next = (zh + (ROWS - g) // ROWS) % 2, (zh + (g + 1) // ROWS) % 2
    prev = ((g + ROWS - 1) % ROWS, x * 4 + z_prev * 2 + core)
    nxt = ((g + 1) % ROWS, x * 4 + z_next * 2 + core)

    near = []
    plane = []
    for dx in (2, 1, 3, 0):
        for dy in (2, 1, 3, 0):
            for dc in (0, 1):
                px, py, pc = (x + dx) % 4, (y + dy) % 4, (core + dc) % 2
                if (dx, dy, dc) != (0, 0, 0):
                    device = (z_lo * 4 + py, px * 4 + zh * 2 + pc)
                    plane.append((device, (px * 2 + pc) * 4 + py))
                    if dy == 0:
                        near.append((device, px * 2 + pc))
    def along(offset):
        at = (zh * 16 + z_lo + offset + 32) % 32
        return ((at % 16) * 4 + y, x * 4 + (at // 16) * 2 + core), at // 16

    near_steps = [(along(-d), d) for d in (1, 2, 3)]
    wide_steps = [(along(d), k) for k, d in ((1, 8), (2, 4), (3, -4))]
    y_peers = [(z_lo * 4 + (y + d) % 4, me) for d in (1, 2, 3)]

    def wide(k):
        return pl.ds(pl.multiple_of(k * 2 * T, 2 * T), 2 * T)

    barrier = pltpu.get_barrier_semaphore()
    everyone = [(g, mate), prev, nxt]
    everyone += [along(d)[0] for d in (1, 2, 3, -8, -4, 4)]
    everyone += [device for device, _ in plane]
    for peer in everyone:
        pl.semaphore_signal(barrier, inc=1, device_id=peer, device_id_type=MESH)
    pl.semaphore_wait(barrier, len(everyone))

    def send(src, dst, send_sem, recv_sem, peer):
        copy = pltpu.make_async_remote_copy(
            src_ref=src,
            dst_ref=dst,
            send_sem=send_sem,
            recv_sem=recv_sem,
            device_id=peer,
            device_id_type=MESH,
        )
        copy.start()
        return copy

    def await_bytes(view, sem):
        pltpu.make_async_copy(view, view, sem).wait()

    step = slots // CHUNKS
    local = [
        pltpu.make_async_copy(src, dst, own_sem.at[k])
        for k, (src, dst) in enumerate(
            (
                (ft, win.at[zh, 1]),
                (ct.at[:, wide(n)], cot_buf.at[me]),
                (cols_h, cols_s),
                (rows_h, rows_s),
                (cols_h, cols_v),
                (rows_h, rows_v),
                (count_h, count_s),
                (w_h, w),
                (bias_h, bias),
            )
        )
    ] + [
        pltpu.make_async_copy(
            tv.at[0, pl.ds(k * step, step)], tvv.at[pl.ds(k * step, step)], tile_sem.at[k]
        )
        for k in range(CHUNKS)
    ]
    for copy in local:
        copy.start()

    half_nodes = ft.shape[1] // 2
    pieces = [pl.ds(k * half_nodes, half_nodes) for k in range(2)]

    def to_sides(src, half, piece):
        there = src.at[:, piece]
        send(there, win.at[half, 0, :, piece], halo_ss.at[half], halo_rs.at[half], nxt)
        send(there, win.at[half, 2, :, piece], halo_ss.at[2 + half], halo_rs.at[2 + half], prev)

    far_ft = [
        send(ft.at[:, piece], win.at[zh, 1, :, piece], far_ss.at[k], far_rs.at[k], (g, mate))
        for k, piece in enumerate(pieces)
    ]
    for piece in pieces:
        to_sides(ft, zh, piece)
    for device, k in near:
        send(ct.at[:, wide(k)], cot_buf.at[me], ss.at[0], rs.at[0], device)
    for copy in far_ft:
        copy.wait_send()
    far_ct = send(ct, cot_far, far_ss.at[2], far_rs.at[2], (g, mate))

    for copy in local:
        copy.wait()

    count = count_s[g]
    live = lax.broadcasted_iota(jnp.int32, (TR, slots), 1) < count
    row_ids = lax.broadcasted_iota(jnp.int32, (TR, slots), 0)
    by_row = jnp.where((rows_v[pl.ds(g, 1), :] == row_ids) & live, 1.0, 0.0).astype(BF16)
    own_cols = cols_v[pl.ds(g, 1), :]
    rel = ((lax.div(own_cols, TR) - g + (ROWS + 1)) % ROWS) * TR + lax.rem(own_cols, TR)
    by_col = [
        jnp.where((rel == row_ids + k * TR) & live, 1.0, 0.0).astype(BF16) for k in range(3)
    ]
    wt[...] = w[...].T
    bias_t[...] = jnp.broadcast_to(bias[...], (2 * T, W * COLS)).T

    def turn(i, _):
        for u in range(8):
            tvt[i * 8 + u] = tvv[i * 8 + u].T
        return 0

    lax.fori_loop(0, slots // 8, turn, 0)
    for k, piece in enumerate(pieces):
        far_ft[k].wait_recv()
        to_sides(win.at[other, 1], other, piece)

    for k in range(4):
        await_bytes(win.at[0, 0], halo_rs.at[k])
    for h in range(2):
        for k in range(3):
            for b in range(TR):
                cols3[k * TR + b, h * W : (h + 1) * W] = win[h, k, :, b * T : (b + 1) * T]

    def forward(i, _):
        for u in range(UNROLL):
            s = i * UNROLL + u
            col = cols_s[g, s]
            grp = jnp.minimum(lax.rem(lax.div(col, TR) - g + (ROWS + 1), ROWS), 2)
            p = dot(cols3[grp * TR + lax.rem(col, TR)], tvt[s])
            prods[pl.ds(pl.multiple_of(s * W2, W2), W2), :] = p
        return 0

    lax.fori_loop(0, slots // UNROLL, forward, 0)
    select_sum(by_row, prods, W2, 0, W2, TR, sums)
    for r in range(TR):
        for h in range(2):
            first = r * W2 + h * W
            agg_send[r // 2, h, r % 2] = sums[first : first + W, :].astype(BF16)
    for device, k in near:
        send(agg_send.at[k], agg_buf.at[x, :, core], ss.at[2], rs.at[2], device)
    far_ct.wait_recv()
    own_cot = pltpu.make_async_copy(cot_far.at[:, wide(n)], cot_buf.at[mate], own_sem.at[1])
    own_cot.start()
    for device, k in near:
        send(cot_far.at[:, wide(k)], cot_buf.at[mate], ss.at[1], rs.at[1], device)
    own_agg = pltpu.make_async_copy(agg_send.at[n], agg_buf.at[x, :, core], own_sem.at[2])
    own_agg.start()
    await_bytes(cot_buf.at[pl.ds(0, 7)], rs.at[0])
    await_bytes(cot_buf.at[pl.ds(0, 7)], rs.at[1])
    own_cot.wait()
    own_agg.wait()
    await_bytes(agg_send.at[pl.ds(0, 7)], rs.at[2])

    agg_t = jnp.concatenate(
        [agg_buf[:, :, :, t].reshape(COLS * W, T) for t in range(2)], axis=1
    )
    pre = dot(wt[...], agg_t) + bias_t[...]
    sigma = jax.nn.sigmoid(pre)
    cot = cot_buf[...].reshape(COLS * W, 2 * T).astype(F32)
    hg = (cot * sigma * (1.0 + pre * (1.0 - sigma))).astype(BF16)
    ag = dot(w[...], hg).astype(BF16)
    for k in range(8):
        for h in range(2):
            first = ((k // 2) * 4 + h * 2 + k % 2) * W
            for t in range(2):
                ag_send[k, t, h] = ag[first : first + W, t * T : (t + 1) * T]
    for device, k in near:
        send(ag_send.at[k], ag_buf.at[pl.ds(2 * n, 2)], ss.at[3], rs.at[3], device)
    own_ag = pltpu.make_async_copy(ag_send.at[n], ag_buf.at[pl.ds(2 * n, 2)], own_sem.at[3])
    own_ag.start()

    wg = dot(agg_t, hg, NT)
    for k in range(8):
        for j in range(4):
            for h in range(2):
                first = ((k // 2) * 4 + h * 2 + k % 2) * W + (j // 2) * 8
                s1_send[k * 4 + j, h] = wg[first : first + 8, (j % 2) * T : (j % 2 + 1) * T]
    bias_rows = dot(jnp.ones((8, 2 * T), BF16), hg, NT)
    bias_tile = jnp.where(
        lax.broadcasted_iota(jnp.int32, (8, 128), 0) < 4, bias_rows[:, 0:128], bias_rows[:, 128:256]
    )
    for k in range(32):
        s1_send[k, 2] = bias_tile
    for device, k in plane:
        send(s1_send.at[k], s1_buf.at[n * 4 + y], ss.at[5], rs.at[5], device)
    s1_buf[pl.ds(n * 4 + y, 1)] = s1_send[pl.ds(n * 4 + y, 1)]
    act_full[...] = (pre * sigma).astype(BF16).reshape(COLS, W, 2 * T)
    for device, k in near:
        send(act_full.at[device[1]], act_buf.at[n], ss.at[4], rs.at[4], device)
    act_buf[pl.ds(n, 1)] = act_full[pl.ds(me, 1)]

    def total(buf, others, k):
        await_bytes(buf.at[pl.ds(0, others)], rs.at[k])
        return jnp.sum(buf[...], axis=0)

    def near_sum():
        value = total(s1_buf, 31, 5)
        r1_send[...] = value
        for (device, _), k in near_steps:
            send(r1_send, r1_buf.at[k - 1], ss.at[6], rs.at[6], device)
        r1_buf[3] = value

    def wide_sum():
        value = total(r1_buf, 3, 6)
        for h in range(2):
            r2_send[h, 0] = value[h]
            r2_send[h, 1] = value[2]
        for (device, half), k in wide_steps:
            send(r2_send.at[half], r2_buf.at[k - 1], ss.at[7], rs.at[7], device)
        r2_buf[pl.ds(3, 1)] = r2_send[pl.ds(zh, 1)]

    def backward(i, _):
        for u in range(UNROLL):
            s = i * UNROLL + u
            p = dot(ag_buf[rows_s[g, s]].reshape(W2, T), tvv[s])
            prods[pl.ds(pl.multiple_of(s * W2, W2), W2), :] = p
        return 0

    await_bytes(ag_send.at[pl.ds(0, 7)], rs.at[3])
    own_ag.wait()
    turns = slots // UNROLL
    lax.fori_loop(0, turns // 2, backward, 0)
    near_sum()
    lax.fori_loop(turns // 2, turns, backward, 0)
    back = []
    for k, (peer, half) in enumerate(((prev, z_prev), (nxt, z_next))):
        select_sum(by_col[2 * k], prods, W2, half * W, W, TR, sums)
        halo_send[k] = sums[0 : TR * W, :].astype(BF16).reshape(TR, W, T)
        back.append(send(halo_send.at[k], halo_buf.at[k], back_ss.at[k], back_rs.at[k], peer))
    wide_sum()
    select_sum(by_col[1], prods, W2, zh * W, W, TR, sums)

    await_bytes(act_buf.at[pl.ds(0, 7)], rs.at[4])
    for k in range(8):
        act_o[:, k * 2 * T : (k + 1) * 2 * T] = act_buf[k]
    for copy in back:
        copy.wait_recv()
    for k in range(TR):
        fg_o[:, k * T : (k + 1) * T] = (
            sums[k * W : (k + 1) * W, :] + halo_buf[0, k].astype(F32) + halo_buf[1, k].astype(F32)
        ).astype(BF16)
    value = total(r2_buf, 3, 7)
    y_send[...] = value
    for device in y_peers:
        send(y_send, y_buf.at[y], ss.at[8], rs.at[8], device)
    y_buf[pl.ds(y, 1)] = value[None]

    far_ct.wait_send()
    for k in range(4):
        await_bytes(win.at[0, 0], halo_ss.at[k])
    for copy in back:
        copy.wait_send()
    for k, view in (
        (0, cot_buf.at[pl.ds(0, 7)]),
        (1, cot_buf.at[pl.ds(0, 7)]),
        (2, agg_send.at[pl.ds(0, 7)]),
        (3, ag_send.at[pl.ds(0, 7)]),
        (4, act_buf.at[pl.ds(0, 7)]),
        (5, s1_buf.at[pl.ds(0, 31)]),
        (6, r1_buf.at[pl.ds(0, 3)]),
        (7, r2_buf.at[pl.ds(0, 3)]),
        (8, y_buf.at[pl.ds(0, 3)]),
    ):
        await_bytes(view, ss.at[k])
    await_bytes(y_buf.at[pl.ds(0, 3)], rs.at[8])
    for j in range(4):
        wg_o[(j // 2) * 8 : (j // 2 + 1) * 8, (j % 2) * T : (j % 2 + 1) * T] = y_buf[j, 0] * scale
    row = jnp.where(me < 8, y_buf[0, 1, 0:1], y_buf[0, 1, 4:5]) * scale
    bg_o[...] = pltpu.roll(row, (128 - (me % 8) * W) % 128, 1)[:, 0:W]


def on_device(features, tile_values, tile_rows, tile_cols, tile_count, weight, out_bias, cotangent):
    slots = tile_values.shape[1]
    nodes = features.shape[0]
    width = weight.shape[0]
    scale = 1.0 / math.sqrt(nodes * ROWS)
    vmem = pl.BlockSpec(memory_space=pltpu.VMEM)
    hbm = pl.BlockSpec(memory_space=pltpu.HBM)
    tiles = lambda *k: pltpu.VMEM(k + (8, T), F32)
    act, fg, wg, bg = pl.pallas_call(
        functools.partial(kernel, slots, scale),
        out_shape=(
            jax.ShapeDtypeStruct((W, nodes), BF16),
            jax.ShapeDtypeStruct((W, nodes), BF16),
            jax.ShapeDtypeStruct((W, width), F32),
            jax.ShapeDtypeStruct((1, W), F32),
        ),
        in_specs=[hbm] * 8,
        out_specs=(vmem,) * 4,
        scratch_shapes=[
            pltpu.SMEM(tile_rows.shape, jnp.int32),
            pltpu.SMEM(tile_cols.shape, jnp.int32),
            pltpu.SMEM(tile_count.shape, jnp.int32),
            pltpu.VMEM(tile_rows.shape, jnp.int32),
            pltpu.VMEM(tile_cols.shape, jnp.int32),
            pltpu.VMEM(weight.shape, BF16),
            pltpu.VMEM((1, width), F32),
            pltpu.VMEM((2, 3, W, nodes), BF16),
            pltpu.VMEM((3 * TR, W2, T), BF16),
            pltpu.VMEM((slots, T, T), BF16),
            pltpu.VMEM((slots, T, T), BF16),
            pltpu.VMEM((slots * W2, T), F32),
            pltpu.VMEM((TR * W2, T), F32),
            pltpu.VMEM((width, width), BF16),
            pltpu.VMEM((width, 2 * T), F32),
            pltpu.VMEM((W, nodes), BF16),
            pltpu.VMEM((COLS, W, 2 * T), BF16),
            pltpu.VMEM((8, 2, 2, W, T), BF16),
            pltpu.VMEM((4, 2, 2, 2, W, T), BF16),
            pltpu.VMEM((8, 2, 2, W, T), BF16),
            pltpu.VMEM((TR, 2, W, T), BF16),
            pltpu.VMEM((COLS, W, 2 * T), BF16),
            pltpu.VMEM((8, W, 2 * T), BF16),
            pltpu.VMEM((2, TR, W, T), BF16),
            pltpu.VMEM((2, TR, W, T), BF16),
            tiles(32, 3),
            tiles(32, 3),
            tiles(3),
            tiles(4, 3),
            tiles(2, 2),
            tiles(4, 2),
            tiles(2),
            tiles(4, 2),
            pltpu.SemaphoreType.DMA((CHUNKS,)),
            pltpu.SemaphoreType.DMA((9,)),
            pltpu.SemaphoreType.DMA((4,)),
            pltpu.SemaphoreType.DMA((4,)),
            pltpu.SemaphoreType.DMA((3,)),
            pltpu.SemaphoreType.DMA((3,)),
            pltpu.SemaphoreType.DMA((2,)),
            pltpu.SemaphoreType.DMA((2,)),
            pltpu.SemaphoreType.DMA((9,)),
            pltpu.SemaphoreType.DMA((9,)),
        ],
        compiler_params=pltpu.CompilerParams(
            collective_id=0, has_side_effects=True, vmem_limit_bytes=32 * 1024 * 1024
        ),
        name="graph_layer",
    )(
        features.T,
        cotangent.T,
        tile_values,
        tile_rows,
        tile_cols,
        tile_count,
        weight,
        out_bias.reshape(1, width),
    )
    return act.T, fg.T, wg, bg.reshape(W)


def solution(mesh):
    in_specs = (
        P("row", "col"),
        P("row", None, None, None),
        P(),
        P(),
        P(),
        P(),
        P(),
        P("row", "col"),
    )
    out_specs = (P("row", "col"), P("row", "col"), P("col", None), P("col"))
    return jax.shard_map(
        on_device, mesh=mesh, in_specs=in_specs, out_specs=out_specs, check_vma=False
    )
```

```python
import functools
import math

import jax
import jax.numpy as jnp
from jax import lax
from jax.experimental import pallas as pl
from jax.experimental.pallas import tpu as pltpu
from jax.sharding import PartitionSpec as P

MESH = pl.DeviceIdType.MESH
F32 = jnp.float32
BF16 = jnp.bfloat16
T = 128
TR = 16
W = 16
W2 = 2 * W
ROWS = 64
COLS = 16
UNROLL = 48
CHUNKS = 4
NT = (((1,), (1,)), ((), ()))
NN = (((1,), (0,)), ((), ()))


def dot(a, b, dims=NN):
    return lax.dot_general(a, b, dims, preferred_element_type=F32)


def select_sum(onehot, prods, stride, first, count, targets, out):
    slots = onehot.shape[1]
    for f in range(count):
        v = prods[pl.ds(first + f, slots, stride=stride), :]
        hi = v.astype(BF16)
        lo = (v - hi.astype(F32)).astype(BF16)
        out[pl.ds(f, targets, stride=count), :] = dot(onehot, hi) + dot(onehot, lo)


def two_products(first, second, tiles):
    none = jnp.zeros_like(first)
    both = jnp.concatenate(
        [jnp.concatenate([first, none], axis=1), jnp.concatenate([none, second], axis=1)], axis=0
    )
    return dot(both, tiles.reshape(2 * T, T))


def kernel(
    slots,
    scale,
    ft,
    ct,
    tv,
    rows_h,
    cols_h,
    count_h,
    w_h,
    bias_h,
    act_o,
    fg_o,
    wg_o,
    bg_o,
    rows_s,
    cols_s,
    count_s,
    rows_v,
    cols_v,
    w,
    bias,
    win,
    cols3,
    tvv,
    tvt,
    prods,
    sums,
    wt,
    bias_t,
    cot_far,
    cot_buf,
    agg_send,
    agg_buf,
    ag_send,
    ag_buf,
    act_full,
    act_buf,
    halo_send,
    halo_buf,
    s1_send,
    s1_buf,
    r1_send,
    r1_buf,
    r2_send,
    r2_buf,
    y_send,
    y_buf,
    tile_sem,
    own_sem,
    halo_ss,
    halo_rs,
    far_ss,
    far_rs,
    back_ss,
    back_rs,
    ss,
    rs,
):
    g = lax.axis_index("row")
    me = lax.axis_index("col")
    z_lo, y = g // 4, g % 4
    x, zh, core = me // 4, (me // 2) % 2, me % 2
    n = x * 2 + core
    other = (zh + 1) % 2
    mate = x * 4 + other * 2 + core
    z_prev, z_next = (zh + (ROWS - g) // ROWS) % 2, (zh + (g + 1) // ROWS) % 2
    prev = ((g + ROWS - 1) % ROWS, x * 4 + z_prev * 2 + core)
    nxt = ((g + 1) % ROWS, x * 4 + z_next * 2 + core)

    near = []
    plane = []
    for dx in (2, 1, 3, 0):
        for dy in (2, 1, 3, 0):
            for dc in (0, 1):
                px, py, pc = (x + dx) % 4, (y + dy) % 4, (core + dc) % 2
                if (dx, dy, dc) != (0, 0, 0):
                    device = (z_lo * 4 + py, px * 4 + zh * 2 + pc)
                    plane.append((device, (px * 2 + pc) * 4 + py))
                    if dy == 0:
                        near.append((device, px * 2 + pc))
    def along(offset):
        at = (zh * 16 + z_lo + offset + 32) % 32
        return ((at % 16) * 4 + y, x * 4 + (at // 16) * 2 + core), at // 16

    near_steps = [(along(-d), d) for d in (1, 2, 3)]
    wide_steps = [(along(d), k) for k, d in ((1, 8), (2, 4), (3, -4))]
    y_peers = [(z_lo * 4 + (y + d) % 4, me) for d in (1, 2, 3)]

    def wide(k):
        return pl.ds(pl.multiple_of(k * 2 * T, 2 * T), 2 * T)

    barrier = pltpu.get_barrier_semaphore()
    everyone = [(g, mate), prev, nxt]
    everyone += [along(d)[0] for d in (1, 2, 3, -8, -4, 4)]
    everyone += [device for device, _ in plane]
    for peer in everyone:
        pl.semaphore_signal(barrier, inc=1, device_id=peer, device_id_type=MESH)
    pl.semaphore_wait(barrier, len(everyone))

    def send(src, dst, send_sem, recv_sem, peer):
        copy = pltpu.make_async_remote_copy(
            src_ref=src,
            dst_ref=dst,
            send_sem=send_sem,
            recv_sem=recv_sem,
            device_id=peer,
            device_id_type=MESH,
        )
        copy.start()
        return copy

    def await_bytes(view, sem):
        pltpu.make_async_copy(view, view, sem).wait()

    step = slots // CHUNKS
    local = [
        pltpu.make_async_copy(src, dst, own_sem.at[k])
        for k, (src, dst) in enumerate(
            (
                (ft, win.at[zh, 1]),
                (ct.at[:, wide(n)], cot_buf.at[me]),
                (cols_h, cols_s),
                (rows_h, rows_s),
                (cols_h, cols_v),
                (rows_h, rows_v),
                (count_h, count_s),
                (w_h, w),
                (bias_h, bias),
            )
        )
    ] + [
        pltpu.make_async_copy(
            tv.at[0, pl.ds(k * step, step)], tvv.at[pl.ds(k * step, step)], tile_sem.at[k]
        )
        for k in range(CHUNKS)
    ]
    for copy in local:
        copy.start()

    half_nodes = ft.shape[1] // 2
    pieces = [pl.ds(k * half_nodes, half_nodes) for k in range(2)]

    def to_sides(src, half, piece):
        there = src.at[:, piece]
        send(there, win.at[half, 0, :, piece], halo_ss.at[half], halo_rs.at[half], nxt)
        send(there, win.at[half, 2, :, piece], halo_ss.at[2 + half], halo_rs.at[2 + half], prev)

    far_ft = [
        send(ft.at[:, piece], win.at[zh, 1, :, piece], far_ss.at[k], far_rs.at[k], (g, mate))
        for k, piece in enumerate(pieces)
    ]
    for piece in pieces:
        to_sides(ft, zh, piece)
    for device, k in near:
        send(ct.at[:, wide(k)], cot_buf.at[me], ss.at[0], rs.at[0], device)

    for copy in local:
        copy.wait()

    count = count_s[g]
    live = lax.broadcasted_iota(jnp.int32, (TR, slots), 1) < count
    row_ids = lax.broadcasted_iota(jnp.int32, (TR, slots), 0)
    by_row = jnp.where((rows_v[pl.ds(g, 1), :] == row_ids) & live, 1.0, 0.0).astype(BF16)
    own_cols = cols_v[pl.ds(g, 1), :]
    rel = ((lax.div(own_cols, TR) - g + (ROWS + 1)) % ROWS) * TR + lax.rem(own_cols, TR)
    by_col = [
        jnp.where((rel == row_ids + k * TR) & live, 1.0, 0.0).astype(BF16) for k in range(3)
    ]
    wt[...] = w[...].T
    bias_t[...] = jnp.broadcast_to(bias[...], (2 * T, W * COLS)).T

    def turn(i, _):
        for u in range(16):
            tvt[i * 16 + u] = tvv[i * 16 + u].T
        return 0

    lax.fori_loop(0, slots // 16, turn, 0)
    for k, piece in enumerate(pieces):
        far_ft[k].wait_recv()
        to_sides(win.at[other, 1], other, piece)
    far_ct = [
        send(ct.at[:, piece], cot_far.at[:, piece], far_ss.at[2 + k], far_rs.at[2 + k], (g, mate))
        for k, piece in enumerate(pieces)
    ]

    for k in range(4):
        await_bytes(win.at[0, 0], halo_rs.at[k])
    for h in range(2):
        for k in range(3):
            for b in range(TR):
                cols3[k * TR + b, h * W : (h + 1) * W] = win[h, k, :, b * T : (b + 1) * T]

    def columns_of(s):
        col = cols_s[g, s]
        grp = jnp.minimum(lax.rem(lax.div(col, TR) - g + (ROWS + 1), ROWS), 2)
        return cols3[grp * TR + lax.rem(col, TR)]

    def forward(i, _):
        for u in range(0, UNROLL, 2):
            s = i * UNROLL + u
            p = two_products(columns_of(s), columns_of(s + 1), tvt[pl.ds(s, 2)])
            prods[pl.ds(pl.multiple_of(s * W2, 2 * W2), 2 * W2), :] = p
        return 0

    lax.fori_loop(0, slots // UNROLL, forward, 0)
    select_sum(by_row, prods, W2, 0, W2, TR, sums)
    for r in range(TR):
        for h in range(2):
            first = r * W2 + h * W
            agg_send[r // 2, h, r % 2] = sums[first : first + W, :].astype(BF16)
    for device, k in near:
        send(agg_send.at[k], agg_buf.at[x, :, core], ss.at[2], rs.at[2], device)
    for copy in far_ct:
        copy.wait_recv()
    own_cot = pltpu.make_async_copy(cot_far.at[:, wide(n)], cot_buf.at[mate], own_sem.at[1])
    own_cot.start()
    for device, k in near:
        send(cot_far.at[:, wide(k)], cot_buf.at[mate], ss.at[1], rs.at[1], device)
    own_agg = pltpu.make_async_copy(agg_send.at[n], agg_buf.at[x, :, core], own_sem.at[2])
    own_agg.start()
    await_bytes(cot_buf.at[pl.ds(0, 7)], rs.at[0])
    await_bytes(cot_buf.at[pl.ds(0, 7)], rs.at[1])
    own_cot.wait()
    own_agg.wait()
    await_bytes(agg_send.at[pl.ds(0, 7)], rs.at[2])

    agg_t = jnp.concatenate(
        [agg_buf[:, :, :, t].reshape(COLS * W, T) for t in range(2)], axis=1
    )
    pre = dot(wt[...], agg_t) + bias_t[...]
    sigma = jax.nn.sigmoid(pre)
    cot = cot_buf[...].reshape(COLS * W, 2 * T).astype(F32)
    hg = (cot * sigma * (1.0 + pre * (1.0 - sigma))).astype(BF16)
    ag = dot(w[...], hg).astype(BF16)
    for k in range(8):
        for h in range(2):
            first = ((k // 2) * 4 + h * 2 + k % 2) * W
            for t in range(2):
                ag_send[k, t, h] = ag[first : first + W, t * T : (t + 1) * T]
    for device, k in near:
        send(ag_send.at[k], ag_buf.at[pl.ds(2 * n, 2)], ss.at[3], rs.at[3], device)
    own_ag = pltpu.make_async_copy(ag_send.at[n], ag_buf.at[pl.ds(2 * n, 2)], own_sem.at[3])
    own_ag.start()

    wg = dot(agg_t, hg, NT)
    for k in range(8):
        for j in range(4):
            for h in range(2):
                first = ((k // 2) * 4 + h * 2 + k % 2) * W + (j // 2) * 8
                s1_send[k * 4 + j, h] = wg[first : first + 8, (j % 2) * T : (j % 2 + 1) * T]
    bias_rows = dot(jnp.ones((8, 2 * T), BF16), hg, NT)
    bias_tile = jnp.where(
        lax.broadcasted_iota(jnp.int32, (8, 128), 0) < 4, bias_rows[:, 0:128], bias_rows[:, 128:256]
    )
    for k in range(32):
        s1_send[k, 2] = bias_tile
    for device, k in plane:
        send(s1_send.at[k], s1_buf.at[n * 4 + y], ss.at[5], rs.at[5], device)
    s1_buf[pl.ds(n * 4 + y, 1)] = s1_send[pl.ds(n * 4 + y, 1)]
    act_full[...] = (pre * sigma).astype(BF16).reshape(COLS, W, 2 * T)
    for device, k in near:
        send(act_full.at[device[1]], act_buf.at[n], ss.at[4], rs.at[4], device)
    act_buf[pl.ds(n, 1)] = act_full[pl.ds(me, 1)]

    def total(buf, others, k):
        await_bytes(buf.at[pl.ds(0, others)], rs.at[k])
        return jnp.sum(buf[...], axis=0)

    def near_sum():
        value = total(s1_buf, 31, 5)
        r1_send[...] = value
        for (device, _), k in near_steps:
            send(r1_send, r1_buf.at[k - 1], ss.at[6], rs.at[6], device)
        r1_buf[3] = value

    def wide_sum():
        value = total(r1_buf, 3, 6)
        for h in range(2):
            r2_send[h, 0] = value[h]
            r2_send[h, 1] = value[2]
        for (device, half), k in wide_steps:
            send(r2_send.at[half], r2_buf.at[k - 1], ss.at[7], rs.at[7], device)
        r2_buf[pl.ds(3, 1)] = r2_send[pl.ds(zh, 1)]

    def backward(i, _):
        for u in range(0, UNROLL, 2):
            s = i * UNROLL + u
            p = two_products(
                ag_buf[rows_s[g, s]].reshape(W2, T),
                ag_buf[rows_s[g, s + 1]].reshape(W2, T),
                tvv[pl.ds(s, 2)],
            )
            prods[pl.ds(pl.multiple_of(s * W2, 2 * W2), 2 * W2), :] = p
        return 0

    await_bytes(ag_send.at[pl.ds(0, 7)], rs.at[3])
    own_ag.wait()
    turns = slots // UNROLL
    lax.fori_loop(0, turns // 2, backward, 0)
    near_sum()
    lax.fori_loop(turns // 2, turns, backward, 0)
    back = []
    for k, (peer, half) in enumerate(((prev, z_prev), (nxt, z_next))):
        select_sum(by_col[2 * k], prods, W2, half * W, W, TR, sums)
        halo_send[k] = sums[0 : TR * W, :].astype(BF16).reshape(TR, W, T)
        back.append(send(halo_send.at[k], halo_buf.at[k], back_ss.at[k], back_rs.at[k], peer))
    wide_sum()
    select_sum(by_col[1], prods, W2, zh * W, W, TR, sums)

    await_bytes(act_buf.at[pl.ds(0, 7)], rs.at[4])
    for k in range(8):
        act_o[:, k * 2 * T : (k + 1) * 2 * T] = act_buf[k]
    for copy in back:
        copy.wait_recv()
    for k in range(TR):
        fg_o[:, k * T : (k + 1) * T] = (
            sums[k * W : (k + 1) * W, :] + halo_buf[0, k].astype(F32) + halo_buf[1, k].astype(F32)
        ).astype(BF16)
    value = total(r2_buf, 3, 7)
    y_send[...] = value
    for device in y_peers:
        send(y_send, y_buf.at[y], ss.at[8], rs.at[8], device)
    y_buf[pl.ds(y, 1)] = value[None]

    for copy in far_ft + far_ct:
        copy.wait_send()
    for k in range(4):
        await_bytes(win.at[0, 0], halo_ss.at[k])
    for copy in back:
        copy.wait_send()
    for k, view in (
        (0, cot_buf.at[pl.ds(0, 7)]),
        (1, cot_buf.at[pl.ds(0, 7)]),
        (2, agg_send.at[pl.ds(0, 7)]),
        (3, ag_send.at[pl.ds(0, 7)]),
        (4, act_buf.at[pl.ds(0, 7)]),
        (5, s1_buf.at[pl.ds(0, 31)]),
        (6, r1_buf.at[pl.ds(0, 3)]),
        (7, r2_buf.at[pl.ds(0, 3)]),
        (8, y_buf.at[pl.ds(0, 3)]),
    ):
        await_bytes(view, ss.at[k])
    await_bytes(y_buf.at[pl.ds(0, 3)], rs.at[8])
    for j in range(4):
        wg_o[(j // 2) * 8 : (j // 2 + 1) * 8, (j % 2) * T : (j % 2 + 1) * T] = y_buf[j, 0] * scale
    row = jnp.where(me < 8, y_buf[0, 1, 0:1], y_buf[0, 1, 4:5]) * scale
    bg_o[...] = pltpu.roll(row, (128 - (me % 8) * W) % 128, 1)[:, 0:W]


def on_device(features, tile_values, tile_rows, tile_cols, tile_count, weight, out_bias, cotangent):
    slots = tile_values.shape[1]
    nodes = features.shape[0]
    width = weight.shape[0]
    scale = 1.0 / math.sqrt(nodes * ROWS)
    vmem = pl.BlockSpec(memory_space=pltpu.VMEM)
    hbm = pl.BlockSpec(memory_space=pltpu.HBM)
    tiles = lambda *k: pltpu.VMEM(k + (8, T), F32)
    act, fg, wg, bg = pl.pallas_call(
        functools.partial(kernel, slots, scale),
        out_shape=(
            jax.ShapeDtypeStruct((W, nodes), BF16),
            jax.ShapeDtypeStruct((W, nodes), BF16),
            jax.ShapeDtypeStruct((W, width), F32),
            jax.ShapeDtypeStruct((1, W), F32),
        ),
        in_specs=[hbm] * 8,
        out_specs=(vmem,) * 4,
        scratch_shapes=[
            pltpu.SMEM(tile_rows.shape, jnp.int32),
            pltpu.SMEM(tile_cols.shape, jnp.int32),
            pltpu.SMEM(tile_count.shape, jnp.int32),
            pltpu.VMEM(tile_rows.shape, jnp.int32),
            pltpu.VMEM(tile_cols.shape, jnp.int32),
            pltpu.VMEM(weight.shape, BF16),
            pltpu.VMEM((1, width), F32),
            pltpu.VMEM((2, 3, W, nodes), BF16),
            pltpu.VMEM((3 * TR, W2, T), BF16),
            pltpu.VMEM((slots, T, T), BF16),
            pltpu.VMEM((slots, T, T), BF16),
            pltpu.VMEM((slots * W2, T), F32),
            pltpu.VMEM((TR * W2, T), F32),
            pltpu.VMEM((width, width), BF16),
            pltpu.VMEM((width, 2 * T), F32),
            pltpu.VMEM((W, nodes), BF16),
            pltpu.VMEM((COLS, W, 2 * T), BF16),
            pltpu.VMEM((8, 2, 2, W, T), BF16),
            pltpu.VMEM((4, 2, 2, 2, W, T), BF16),
            pltpu.VMEM((8, 2, 2, W, T), BF16),
            pltpu.VMEM((TR, 2, W, T), BF16),
            pltpu.VMEM((COLS, W, 2 * T), BF16),
            pltpu.VMEM((8, W, 2 * T), BF16),
            pltpu.VMEM((2, TR, W, T), BF16),
            pltpu.VMEM((2, TR, W, T), BF16),
            tiles(32, 3),
            tiles(32, 3),
            tiles(3),
            tiles(4, 3),
            tiles(2, 2),
            tiles(4, 2),
            tiles(2),
            tiles(4, 2),
            pltpu.SemaphoreType.DMA((CHUNKS,)),
            pltpu.SemaphoreType.DMA((9,)),
            pltpu.SemaphoreType.DMA((4,)),
            pltpu.SemaphoreType.DMA((4,)),
            pltpu.SemaphoreType.DMA((4,)),
            pltpu.SemaphoreType.DMA((4,)),
            pltpu.SemaphoreType.DMA((2,)),
            pltpu.SemaphoreType.DMA((2,)),
            pltpu.SemaphoreType.DMA((9,)),
            pltpu.SemaphoreType.DMA((9,)),
        ],
        compiler_params=pltpu.CompilerParams(
            collective_id=0, has_side_effects=True, vmem_limit_bytes=32 * 1024 * 1024
        ),
        name="graph_layer",
    )(
        features.T,
        cotangent.T,
        tile_values,
        tile_rows,
        tile_cols,
        tile_count,
        weight,
        out_bias.reshape(1, width),
    )
    return act.T, fg.T, wg, bg.reshape(W)


def solution(mesh):
    in_specs = (
        P("row", "col"),
        P("row", None, None, None),
        P(),
        P(),
        P(),
        P(),
        P(),
        P("row", "col"),
    )
    out_specs = (P("row", "col"), P("row", "col"), P("col", None), P("col"))
    return jax.shard_map(
        on_device, mesh=mesh, in_specs=in_specs, out_specs=out_specs, check_vma=False
    )
```

```python
import functools
import math

import jax
import jax.numpy as jnp
from jax import lax
from jax.experimental import pallas as pl
from jax.experimental.pallas import tpu as pltpu
from jax.sharding import PartitionSpec as P

MESH = pl.DeviceIdType.MESH
F32 = jnp.float32
BF16 = jnp.bfloat16
T = 128
TR = 16
W = 16
W2 = 2 * W
ROWS = 64
COLS = 16
UNROLL = 48
CHUNKS = 4
NT = (((1,), (1,)), ((), ()))
NN = (((1,), (0,)), ((), ()))


def dot(a, b, dims=NN):
    return lax.dot_general(a, b, dims, preferred_element_type=F32)


def select_sum(onehot, prods, stride, first, count, targets, out):
    slots = onehot.shape[1]
    for f in range(count):
        v = prods[pl.ds(first + f, slots, stride=stride), :]
        hi = v.astype(BF16)
        lo = (v - hi.astype(F32)).astype(BF16)
        out[pl.ds(f, targets, stride=count), :] = dot(onehot, hi) + dot(onehot, lo)


def two_products(first, second, tiles):
    none = jnp.zeros_like(first)
    both = jnp.concatenate(
        [jnp.concatenate([first, none], axis=1), jnp.concatenate([none, second], axis=1)], axis=0
    )
    return dot(both, tiles.reshape(2 * T, T))


def kernel(
    slots,
    scale,
    ft,
    ct,
    tv,
    rows_h,
    cols_h,
    count_h,
    w_h,
    bias_h,
    act_o,
    fg_o,
    wg_o,
    bg_o,
    rows_s,
    cols_s,
    count_s,
    rows_v,
    cols_v,
    w,
    bias,
    win,
    cols3,
    tvv,
    tvt,
    prods,
    sums,
    wt,
    bias_t,
    cot_far,
    cot_buf,
    agg_send,
    agg_buf,
    ag_send,
    ag_buf,
    act_full,
    act_buf,
    halo_send,
    halo_buf,
    s1_send,
    s1_buf,
    bias_send,
    bias_buf,
    r1_send,
    r1_buf,
    r2_send,
    r2_buf,
    y_send,
    y_buf,
    tile_sem,
    own_sem,
    halo_ss,
    halo_rs,
    far_ss,
    far_rs,
    back_ss,
    back_rs,
    ss,
    rs,
):
    g = lax.axis_index("row")
    me = lax.axis_index("col")
    z_lo, y = g // 4, g % 4
    x, zh, core = me // 4, (me // 2) % 2, me % 2
    n = x * 2 + core
    other = (zh + 1) % 2
    mate = x * 4 + other * 2 + core
    z_prev, z_next = (zh + (ROWS - g) // ROWS) % 2, (zh + (g + 1) // ROWS) % 2
    prev = ((g + ROWS - 1) % ROWS, x * 4 + z_prev * 2 + core)
    nxt = ((g + 1) % ROWS, x * 4 + z_next * 2 + core)

    near = []
    plane = []
    for dx in (2, 1, 3, 0):
        for dy in (2, 1, 3, 0):
            for dc in (0, 1):
                px, py, pc = (x + dx) % 4, (y + dy) % 4, (core + dc) % 2
                if (dx, dy, dc) != (0, 0, 0):
                    device = (z_lo * 4 + py, px * 4 + zh * 2 + pc)
                    plane.append((device, (px * 2 + pc) * 4 + py))
                    if dy == 0:
                        near.append((device, px * 2 + pc))
    def along(offset):
        at = (zh * 16 + z_lo + offset + 32) % 32
        return ((at % 16) * 4 + y, x * 4 + (at // 16) * 2 + core), at // 16

    near_steps = [(along(-d), d) for d in (1, 2, 3)]
    wide_steps = [(along(d), k) for k, d in ((1, 8), (2, 4), (3, -4))]
    y_peers = [(z_lo * 4 + (y + d) % 4, me) for d in (1, 2, 3)]

    def wide(k):
        return pl.ds(pl.multiple_of(k * 2 * T, 2 * T), 2 * T)

    barrier = pltpu.get_barrier_semaphore()
    everyone = [(g, mate), prev, nxt]
    everyone += [along(d)[0] for d in (1, 2, 3, -8, -4, 4)]
    everyone += [device for device, _ in plane]
    for peer in everyone:
        pl.semaphore_signal(barrier, inc=1, device_id=peer, device_id_type=MESH)
    pl.semaphore_wait(barrier, len(everyone))

    def send(src, dst, send_sem, recv_sem, peer):
        copy = pltpu.make_async_remote_copy(
            src_ref=src,
            dst_ref=dst,
            send_sem=send_sem,
            recv_sem=recv_sem,
            device_id=peer,
            device_id_type=MESH,
        )
        copy.start()
        return copy

    def await_bytes(view, sem):
        pltpu.make_async_copy(view, view, sem).wait()

    step = slots // CHUNKS
    local = [
        pltpu.make_async_copy(src, dst, own_sem.at[k])
        for k, (src, dst) in enumerate(
            (
                (ft, win.at[zh, 1]),
                (ct.at[:, wide(n)], cot_buf.at[me]),
                (cols_h, cols_s),
                (rows_h, rows_s),
                (cols_h, cols_v),
                (rows_h, rows_v),
                (count_h, count_s),
                (w_h, w),
                (bias_h, bias),
            )
        )
    ] + [
        pltpu.make_async_copy(
            tv.at[0, pl.ds(k * step, step)], tvv.at[pl.ds(k * step, step)], tile_sem.at[k]
        )
        for k in range(CHUNKS)
    ]
    for copy in local:
        copy.start()

    half_nodes = ft.shape[1] // 2
    pieces = [pl.ds(k * half_nodes, half_nodes) for k in range(2)]

    def to_sides(src, half, piece):
        there = src.at[:, piece]
        send(there, win.at[half, 0, :, piece], halo_ss.at[half], halo_rs.at[half], nxt)
        send(there, win.at[half, 2, :, piece], halo_ss.at[2 + half], halo_rs.at[2 + half], prev)

    far_ft = [
        send(ft.at[:, piece], win.at[zh, 1, :, piece], far_ss.at[k], far_rs.at[k], (g, mate))
        for k, piece in enumerate(pieces)
    ]
    for piece in pieces:
        to_sides(ft, zh, piece)
    for device, k in near:
        send(ct.at[:, wide(k)], cot_buf.at[me], ss.at[0], rs.at[0], device)

    for copy in local:
        copy.wait()

    count = count_s[g]
    live = lax.broadcasted_iota(jnp.int32, (TR, slots), 1) < count
    row_ids = lax.broadcasted_iota(jnp.int32, (TR, slots), 0)
    by_row = jnp.where((rows_v[pl.ds(g, 1), :] == row_ids) & live, 1.0, 0.0).astype(BF16)
    own_cols = cols_v[pl.ds(g, 1), :]
    rel = ((lax.div(own_cols, TR) - g + (ROWS + 1)) % ROWS) * TR + lax.rem(own_cols, TR)
    by_col = [
        jnp.where((rel == row_ids + k * TR) & live, 1.0, 0.0).astype(BF16) for k in range(3)
    ]
    wt[...] = w[...].T
    bias_t[...] = jnp.broadcast_to(bias[...], (2 * T, W * COLS)).T

    def turn(i, _):
        for u in range(16):
            tvt[i * 16 + u] = tvv[i * 16 + u].T
        return 0

    lax.fori_loop(0, slots // 16, turn, 0)
    far_ct = [
        send(ct.at[:, piece], cot_far.at[:, piece], far_ss.at[2 + k], far_rs.at[2 + k], (g, mate))
        for k, piece in enumerate(pieces)
    ]
    for k, piece in enumerate(pieces):
        far_ft[k].wait_recv()
        to_sides(win.at[other, 1], other, piece)

    for k in range(4):
        await_bytes(win.at[0, 0], halo_rs.at[k])
    for h in range(2):
        for k in range(3):
            for b in range(TR):
                cols3[k * TR + b, h * W : (h + 1) * W] = win[h, k, :, b * T : (b + 1) * T]

    def columns_of(s):
        col = cols_s[g, s]
        grp = jnp.minimum(lax.rem(lax.div(col, TR) - g + (ROWS + 1), ROWS), 2)
        return cols3[grp * TR + lax.rem(col, TR)]

    def forward(i, _):
        for u in range(0, UNROLL, 2):
            s = i * UNROLL + u
            p = two_products(columns_of(s), columns_of(s + 1), tvt[pl.ds(s, 2)])
            prods[pl.ds(pl.multiple_of(s * W2, 2 * W2), 2 * W2), :] = p
        return 0

    lax.fori_loop(0, slots // UNROLL, forward, 0)
    select_sum(by_row, prods, W2, 0, W2, TR, sums)
    for r in range(TR):
        for h in range(2):
            first = r * W2 + h * W
            agg_send[r // 2, h, r % 2] = sums[first : first + W, :].astype(BF16)
    for device, k in near:
        send(agg_send.at[k], agg_buf.at[x, :, core], ss.at[2], rs.at[2], device)
    for copy in far_ct:
        copy.wait_recv()
    own_cot = pltpu.make_async_copy(cot_far.at[:, wide(n)], cot_buf.at[mate], own_sem.at[1])
    own_cot.start()
    for device, k in near:
        send(cot_far.at[:, wide(k)], cot_buf.at[mate], ss.at[1], rs.at[1], device)
    own_agg = pltpu.make_async_copy(agg_send.at[n], agg_buf.at[x, :, core], own_sem.at[2])
    own_agg.start()
    await_bytes(cot_buf.at[pl.ds(0, 7)], rs.at[0])
    await_bytes(cot_buf.at[pl.ds(0, 7)], rs.at[1])
    own_cot.wait()
    own_agg.wait()
    await_bytes(agg_send.at[pl.ds(0, 7)], rs.at[2])

    agg_t = jnp.concatenate(
        [agg_buf[:, :, :, t].reshape(COLS * W, T) for t in range(2)], axis=1
    )
    pre = dot(wt[...], agg_t) + bias_t[...]
    sigma = jax.nn.sigmoid(pre)
    cot = cot_buf[...].reshape(COLS * W, 2 * T).astype(F32)
    hg = (cot * sigma * (1.0 + pre * (1.0 - sigma))).astype(BF16)
    ag = dot(w[...], hg).astype(BF16)
    for k in range(8):
        for h in range(2):
            first = ((k // 2) * 4 + h * 2 + k % 2) * W
            for t in range(2):
                ag_send[k, t, h] = ag[first : first + W, t * T : (t + 1) * T]
    for device, k in near:
        send(ag_send.at[k], ag_buf.at[pl.ds(2 * n, 2)], ss.at[3], rs.at[3], device)
    own_ag = pltpu.make_async_copy(ag_send.at[n], ag_buf.at[pl.ds(2 * n, 2)], own_sem.at[3])
    own_ag.start()

    wg = dot(agg_t, hg, NT)
    for k in range(8):
        for j in range(4):
            first = ((k // 2) * 4 + k % 2) * W + (j // 2) * 8
            across = slice((j % 2) * T, (j % 2 + 1) * T)
            s1_send[k * 4 + j] = jnp.concatenate(
                [wg[first : first + 8, across], wg[first + 2 * W : first + 2 * W + 8, across]], axis=0
            ).astype(BF16)
    for device, k in plane:
        send(s1_send.at[k], s1_buf.at[n * 4 + y], ss.at[5], rs.at[5], device)
    s1_buf[pl.ds(n * 4 + y, 1)] = s1_send[pl.ds(n * 4 + y, 1)]
    bias_rows = dot(jnp.ones((8, 2 * T), BF16), hg, NT)
    bias_tile = jnp.where(
        lax.broadcasted_iota(jnp.int32, (8, 128), 0) < 4, bias_rows[:, 0:128], bias_rows[:, 128:256]
    )
    bias_send[...] = bias_tile
    for device, k in near:
        send(bias_send, bias_buf.at[n], ss.at[9], rs.at[9], device)
    bias_buf[pl.ds(n, 1)] = bias_tile[None]
    act_full[...] = (pre * sigma).astype(BF16).reshape(COLS, W, 2 * T)
    for device, k in near:
        send(act_full.at[device[1]], act_buf.at[n], ss.at[4], rs.at[4], device)
    act_buf[pl.ds(n, 1)] = act_full[pl.ds(me, 1)]

    def total(buf, others, k):
        await_bytes(buf.at[pl.ds(0, others)], rs.at[k])
        return jnp.sum(buf[...].astype(F32), axis=0)

    def near_sum():
        value = jnp.concatenate([total(s1_buf, 31, 5), total(bias_buf, 7, 9)], axis=0).reshape(3, 8, T)
        r1_send[...] = value
        for (device, _), k in near_steps:
            send(r1_send, r1_buf.at[k - 1], ss.at[6], rs.at[6], device)
        r1_buf[3] = value

    def wide_sum():
        value = total(r1_buf, 3, 6)
        for h in range(2):
            r2_send[h, 0] = value[h]
            r2_send[h, 1] = value[2]
        for (device, half), k in wide_steps:
            send(r2_send.at[half], r2_buf.at[k - 1], ss.at[7], rs.at[7], device)
        r2_buf[pl.ds(3, 1)] = r2_send[pl.ds(zh, 1)]

    def backward(i, _):
        for u in range(0, UNROLL, 2):
            s = i * UNROLL + u
            p = two_products(
                ag_buf[rows_s[g, s]].reshape(W2, T),
                ag_buf[rows_s[g, s + 1]].reshape(W2, T),
                tvv[pl.ds(s, 2)],
            )
            prods[pl.ds(pl.multiple_of(s * W2, 2 * W2), 2 * W2), :] = p
        return 0

    await_bytes(ag_send.at[pl.ds(0, 7)], rs.at[3])
    own_ag.wait()
    turns = slots // UNROLL
    near_sum()
    lax.fori_loop(0, turns, backward, 0)
    wide_sum()
    back = []
    for k, (peer, half) in enumerate(((prev, z_prev), (nxt, z_next))):
        select_sum(by_col[2 * k], prods, W2, half * W, W, TR, sums)
        halo_send[k] = sums[0 : TR * W, :].astype(BF16).reshape(TR, W, T)
        back.append(send(halo_send.at[k], halo_buf.at[k], back_ss.at[k], back_rs.at[k], peer))
    select_sum(by_col[1], prods, W2, zh * W, W, TR, sums)

    await_bytes(act_buf.at[pl.ds(0, 7)], rs.at[4])
    for k in range(8):
        act_o[:, k * 2 * T : (k + 1) * 2 * T] = act_buf[k]
    for copy in back:
        copy.wait_recv()
    for k in range(TR):
        fg_o[:, k * T : (k + 1) * T] = (
            sums[k * W : (k + 1) * W, :] + halo_buf[0, k].astype(F32) + halo_buf[1, k].astype(F32)
        ).astype(BF16)
    value = total(r2_buf, 3, 7)
    y_send[...] = value
    for device in y_peers:
        send(y_send, y_buf.at[y], ss.at[8], rs.at[8], device)
    y_buf[pl.ds(y, 1)] = value[None]

    for copy in far_ft + far_ct:
        copy.wait_send()
    for k in range(4):
        await_bytes(win.at[0, 0], halo_ss.at[k])
    for copy in back:
        copy.wait_send()
    for k, view in (
        (0, cot_buf.at[pl.ds(0, 7)]),
        (1, cot_buf.at[pl.ds(0, 7)]),
        (2, agg_send.at[pl.ds(0, 7)]),
        (3, ag_send.at[pl.ds(0, 7)]),
        (4, act_buf.at[pl.ds(0, 7)]),
        (5, s1_buf.at[pl.ds(0, 31)]),
        (6, r1_buf.at[pl.ds(0, 3)]),
        (7, r2_buf.at[pl.ds(0, 3)]),
        (8, y_buf.at[pl.ds(0, 3)]),
        (9, bias_buf.at[pl.ds(0, 7)]),
    ):
        await_bytes(view, ss.at[k])
    await_bytes(y_buf.at[pl.ds(0, 3)], rs.at[8])
    for j in range(4):
        wg_o[(j // 2) * 8 : (j // 2 + 1) * 8, (j % 2) * T : (j % 2 + 1) * T] = y_buf[j, 0] * scale
    bias_sum = jnp.sum(y_buf[:, 1], axis=0)
    row = jnp.where(me < 8, bias_sum[0:1], bias_sum[4:5]) * scale
    bg_o[...] = pltpu.roll(row, (128 - (me % 8) * W) % 128, 1)[:, 0:W]


def on_device(features, tile_values, tile_rows, tile_cols, tile_count, weight, out_bias, cotangent):
    slots = tile_values.shape[1]
    nodes = features.shape[0]
    width = weight.shape[0]
    scale = 1.0 / math.sqrt(nodes * ROWS)
    vmem = pl.BlockSpec(memory_space=pltpu.VMEM)
    hbm = pl.BlockSpec(memory_space=pltpu.HBM)
    tiles = lambda *k: pltpu.VMEM(k + (8, T), F32)
    act, fg, wg, bg = pl.pallas_call(
        functools.partial(kernel, slots, scale),
        out_shape=(
            jax.ShapeDtypeStruct((W, nodes), BF16),
            jax.ShapeDtypeStruct((W, nodes), BF16),
            jax.ShapeDtypeStruct((W, width), F32),
            jax.ShapeDtypeStruct((1, W), F32),
        ),
        in_specs=[hbm] * 8,
        out_specs=(vmem,) * 4,
        scratch_shapes=[
            pltpu.SMEM(tile_rows.shape, jnp.int32),
            pltpu.SMEM(tile_cols.shape, jnp.int32),
            pltpu.SMEM(tile_count.shape, jnp.int32),
            pltpu.VMEM(tile_rows.shape, jnp.int32),
            pltpu.VMEM(tile_cols.shape, jnp.int32),
            pltpu.VMEM(weight.shape, BF16),
            pltpu.VMEM((1, width), F32),
            pltpu.VMEM((2, 3, W, nodes), BF16),
            pltpu.VMEM((3 * TR, W2, T), BF16),
            pltpu.VMEM((slots, T, T), BF16),
            pltpu.VMEM((slots, T, T), BF16),
            pltpu.VMEM((slots * W2, T), F32),
            pltpu.VMEM((TR * W2, T), F32),
            pltpu.VMEM((width, width), BF16),
            pltpu.VMEM((width, 2 * T), F32),
            pltpu.VMEM((W, nodes), BF16),
            pltpu.VMEM((COLS, W, 2 * T), BF16),
            pltpu.VMEM((8, 2, 2, W, T), BF16),
            pltpu.VMEM((4, 2, 2, 2, W, T), BF16),
            pltpu.VMEM((8, 2, 2, W, T), BF16),
            pltpu.VMEM((TR, 2, W, T), BF16),
            pltpu.VMEM((COLS, W, 2 * T), BF16),
            pltpu.VMEM((8, W, 2 * T), BF16),
            pltpu.VMEM((2, TR, W, T), BF16),
            pltpu.VMEM((2, TR, W, T), BF16),
            pltpu.VMEM((32, W, T), BF16),
            pltpu.VMEM((32, W, T), BF16),
            tiles(),
            tiles(8),
            tiles(3),
            tiles(4, 3),
            tiles(2, 2),
            tiles(4, 2),
            tiles(2),
            tiles(4, 2),
            pltpu.SemaphoreType.DMA((CHUNKS,)),
            pltpu.SemaphoreType.DMA((9,)),
            pltpu.SemaphoreType.DMA((4,)),
            pltpu.SemaphoreType.DMA((4,)),
            pltpu.SemaphoreType.DMA((4,)),
            pltpu.SemaphoreType.DMA((4,)),
            pltpu.SemaphoreType.DMA((2,)),
            pltpu.SemaphoreType.DMA((2,)),
            pltpu.SemaphoreType.DMA((10,)),
            pltpu.SemaphoreType.DMA((10,)),
        ],
        compiler_params=pltpu.CompilerParams(
            collective_id=0, has_side_effects=True, vmem_limit_bytes=32 * 1024 * 1024
        ),
        name="graph_layer",
    )(
        features.T,
        cotangent.T,
        tile_values,
        tile_rows,
        tile_cols,
        tile_count,
        weight,
        out_bias.reshape(1, width),
    )
    return act.T, fg.T, wg, bg.reshape(W)


def solution(mesh):
    in_specs = (
        P("row", "col"),
        P("row", None, None, None),
        P(),
        P(),
        P(),
        P(),
        P(),
        P("row", "col"),
    )
    out_specs = (P("row", "col"), P("row", "col"), P("col", None), P("col"))
    return jax.shard_map(
        on_device, mesh=mesh, in_specs=in_specs, out_specs=out_specs, check_vma=False
    )
```

```python
import functools
import math

import jax
import jax.numpy as jnp
from jax import lax
from jax.experimental import pallas as pl
from jax.experimental.pallas import tpu as pltpu
from jax.sharding import PartitionSpec as P

MESH = pl.DeviceIdType.MESH
F32 = jnp.float32
BF16 = jnp.bfloat16
T = 128
TR = 16
W = 16
W2 = 2 * W
ROWS = 64
COLS = 16
UNROLL = 48
CHUNKS = 4
PIECES = 4
NT = (((1,), (1,)), ((), ()))
NN = (((1,), (0,)), ((), ()))


def dot(a, b, dims=NN):
    return lax.dot_general(a, b, dims, preferred_element_type=F32)


def select_sum(onehot, prods, stride, first, count, targets, out):
    slots = onehot.shape[1]
    for f in range(count):
        v = prods[pl.ds(first + f, slots, stride=stride), :]
        hi = v.astype(BF16)
        lo = (v - hi.astype(F32)).astype(BF16)
        out[pl.ds(f, targets, stride=count), :] = dot(onehot, hi) + dot(onehot, lo)


def two_products(first, second, tiles):
    none = jnp.zeros_like(first)
    both = jnp.concatenate(
        [jnp.concatenate([first, none], axis=1), jnp.concatenate([none, second], axis=1)], axis=0
    )
    return dot(both, tiles.reshape(2 * T, T))


def kernel(
    slots,
    scale,
    ft,
    ct,
    tv,
    rows_h,
    cols_h,
    count_h,
    w_h,
    bias_h,
    act_o,
    fg_o,
    wg_o,
    bg_o,
    rows_s,
    cols_s,
    count_s,
    rows_v,
    cols_v,
    w,
    bias,
    win,
    cols3,
    tvv,
    tvt,
    prods,
    sums,
    wt,
    bias_t,
    cot_far,
    cot_buf,
    agg_send,
    agg_buf,
    ag_send,
    ag_buf,
    act_full,
    act_buf,
    halo_send,
    halo_buf,
    s1_send,
    s1_buf,
    bias_send,
    bias_buf,
    ring_send,
    ring_buf,
    y_send,
    y_buf,
    tile_sem,
    own_sem,
    halo_ss,
    halo_rs,
    far_ss,
    far_rs,
    back_ss,
    back_rs,
    ss,
    rs,
):
    g = lax.axis_index("row")
    me = lax.axis_index("col")
    z_lo, y = g // 4, g % 4
    x, zh, core = me // 4, (me // 2) % 2, me % 2
    n = x * 2 + core
    other = (zh + 1) % 2
    mate = x * 4 + other * 2 + core
    z_prev, z_next = (zh + (ROWS - g) // ROWS) % 2, (zh + (g + 1) // ROWS) % 2
    prev = ((g + ROWS - 1) % ROWS, x * 4 + z_prev * 2 + core)
    nxt = ((g + 1) % ROWS, x * 4 + z_next * 2 + core)

    near = []
    plane = []
    for dx in (2, 1, 3, 0):
        for dy in (2, 1, 3, 0):
            for dc in (0, 1):
                px, py, pc = (x + dx) % 4, (y + dy) % 4, (core + dc) % 2
                if (dx, dy, dc) != (0, 0, 0):
                    device = (z_lo * 4 + py, px * 4 + zh * 2 + pc)
                    plane.append((device, (px * 2 + pc) * 4 + py))
                    if dy == 0:
                        near.append((device, px * 2 + pc))
    def along(offset):
        at = (zh * 16 + z_lo + offset + 32) % 32
        return ((at % 16) * 4 + y, x * 4 + (at // 16) * 2 + core), at // 16

    offsets = (-8, 7, -7, 6, -6, 5, -5, 4, -4, 3, -3, 2, -2, 1, -1)
    y_peers = [(z_lo * 4 + (y + d) % 4, me) for d in (1, 2, 3)]

    def wide(k):
        return pl.ds(pl.multiple_of(k * 2 * T, 2 * T), 2 * T)

    barrier = pltpu.get_barrier_semaphore()
    everyone = [(g, mate), prev, nxt]
    everyone += [along(-d)[0] for d in offsets]
    everyone += [device for device, _ in plane]
    for peer in everyone:
        pl.semaphore_signal(barrier, inc=1, device_id=peer, device_id_type=MESH)
    pl.semaphore_wait(barrier, len(everyone))

    def send(src, dst, send_sem, recv_sem, peer):
        copy = pltpu.make_async_remote_copy(
            src_ref=src,
            dst_ref=dst,
            send_sem=send_sem,
            recv_sem=recv_sem,
            device_id=peer,
            device_id_type=MESH,
        )
        copy.start()
        return copy

    def await_bytes(view, sem):
        pltpu.make_async_copy(view, view, sem).wait()

    step = slots // CHUNKS
    local = [
        pltpu.make_async_copy(src, dst, own_sem.at[k])
        for k, (src, dst) in enumerate(
            (
                (ft, win.at[zh, 1]),
                (ct.at[:, wide(n)], cot_buf.at[me]),
                (cols_h, cols_s),
                (rows_h, rows_s),
                (cols_h, cols_v),
                (rows_h, rows_v),
                (count_h, count_s),
                (w_h, w),
                (bias_h, bias),
            )
        )
    ] + [
        pltpu.make_async_copy(
            tv.at[0, pl.ds(k * step, step)], tvv.at[pl.ds(k * step, step)], tile_sem.at[k]
        )
        for k in range(CHUNKS)
    ]
    for copy in local:
        copy.start()

    cut = ft.shape[1] // PIECES
    pieces = [pl.ds(k * cut, cut) for k in range(PIECES)]

    def to_sides(src, half, piece):
        there = src.at[:, piece]
        send(there, win.at[half, 0, :, piece], halo_ss.at[half], halo_rs.at[half], nxt)
        send(there, win.at[half, 2, :, piece], halo_ss.at[2 + half], halo_rs.at[2 + half], prev)

    far_ft = [
        send(ft.at[:, piece], win.at[zh, 1, :, piece], far_ss.at[k], far_rs.at[k], (g, mate))
        for k, piece in enumerate(pieces)
    ]
    to_sides(ft, zh, pl.ds(0, ft.shape[1]))
    for device, k in near:
        send(ct.at[:, wide(k)], cot_buf.at[me], ss.at[0], rs.at[0], device)

    for copy in local:
        copy.wait()

    count = count_s[g]
    live = lax.broadcasted_iota(jnp.int32, (TR, slots), 1) < count
    row_ids = lax.broadcasted_iota(jnp.int32, (TR, slots), 0)
    by_row = jnp.where((rows_v[pl.ds(g, 1), :] == row_ids) & live, 1.0, 0.0).astype(BF16)
    own_cols = cols_v[pl.ds(g, 1), :]
    rel = ((lax.div(own_cols, TR) - g + (ROWS + 1)) % ROWS) * TR + lax.rem(own_cols, TR)
    by_col = [
        jnp.where((rel == row_ids + k * TR) & live, 1.0, 0.0).astype(BF16) for k in range(3)
    ]
    wt[...] = w[...].T
    bias_t[...] = jnp.broadcast_to(bias[...], (2 * T, W * COLS)).T

    def turn(i, _):
        for u in range(16):
            tvt[i * 16 + u] = tvv[i * 16 + u].T
        return 0

    lax.fori_loop(0, slots // 16, turn, 0)
    far_ct = send(ct, cot_far, far_ss.at[PIECES], far_rs.at[PIECES], (g, mate))
    for k, piece in enumerate(pieces):
        far_ft[k].wait_recv()
        to_sides(win.at[other, 1], other, piece)

    for k in range(4):
        await_bytes(win.at[0, 0], halo_rs.at[k])
    for h in range(2):
        for k in range(3):
            for b in range(TR):
                cols3[k * TR + b, h * W : (h + 1) * W] = win[h, k, :, b * T : (b + 1) * T]

    def columns_of(s):
        col = cols_s[g, s]
        grp = jnp.minimum(lax.rem(lax.div(col, TR) - g + (ROWS + 1), ROWS), 2)
        return cols3[grp * TR + lax.rem(col, TR)]

    def forward(i, _):
        for u in range(0, UNROLL, 2):
            s = i * UNROLL + u
            p = two_products(columns_of(s), columns_of(s + 1), tvt[pl.ds(s, 2)])
            prods[pl.ds(pl.multiple_of(s * W2, 2 * W2), 2 * W2), :] = p
        return 0

    lax.fori_loop(0, slots // UNROLL, forward, 0)
    for h in range(2):
        select_sum(by_row, prods, W2, h * W, W, TR, sums)
        for r in range(TR):
            agg_send[r // 2, h, r % 2] = sums[r * W : (r + 1) * W, :].astype(BF16)
        for device, k in near:
            send(agg_send.at[k, h], agg_buf.at[x, h, core], ss.at[2], rs.at[2], device)
    far_ct.wait_recv()
    own_cot = pltpu.make_async_copy(cot_far.at[:, wide(n)], cot_buf.at[mate], own_sem.at[1])
    own_cot.start()
    for device, k in near:
        send(cot_far.at[:, wide(k)], cot_buf.at[mate], ss.at[1], rs.at[1], device)
    own_agg = pltpu.make_async_copy(agg_send.at[n], agg_buf.at[x, :, core], own_sem.at[2])
    own_agg.start()
    await_bytes(cot_buf.at[pl.ds(0, 7)], rs.at[0])
    await_bytes(cot_buf.at[pl.ds(0, 7)], rs.at[1])
    own_cot.wait()
    own_agg.wait()
    await_bytes(agg_send.at[pl.ds(0, 7)], rs.at[2])

    agg_t = jnp.concatenate(
        [agg_buf[:, :, :, t].reshape(COLS * W, T) for t in range(2)], axis=1
    )
    pre = dot(wt[...], agg_t) + bias_t[...]
    sigma = jax.nn.sigmoid(pre)
    cot = cot_buf[...].reshape(COLS * W, 2 * T).astype(F32)
    hg = (cot * sigma * (1.0 + pre * (1.0 - sigma))).astype(BF16)
    ag = dot(w[...], hg).astype(BF16)
    for k in range(8):
        for h in range(2):
            first = ((k // 2) * 4 + h * 2 + k % 2) * W
            for t in range(2):
                ag_send[k, t, h] = ag[first : first + W, t * T : (t + 1) * T]
    for device, k in near:
        send(ag_send.at[k], ag_buf.at[pl.ds(2 * n, 2)], ss.at[3], rs.at[3], device)
    own_ag = pltpu.make_async_copy(ag_send.at[n], ag_buf.at[pl.ds(2 * n, 2)], own_sem.at[3])
    own_ag.start()

    wg = dot(agg_t, hg, NT)
    for k in range(8):
        for j in range(4):
            first = ((k // 2) * 4 + k % 2) * W + (j // 2) * 8
            across = slice((j % 2) * T, (j % 2 + 1) * T)
            s1_send[k * 4 + j] = jnp.concatenate(
                [wg[first : first + 8, across], wg[first + 2 * W : first + 2 * W + 8, across]], axis=0
            ).astype(BF16)
    for device, k in plane:
        send(s1_send.at[k], s1_buf.at[n * 4 + y], ss.at[5], rs.at[5], device)
    s1_buf[pl.ds(n * 4 + y, 1)] = s1_send[pl.ds(n * 4 + y, 1)]
    bias_rows = dot(jnp.ones((8, 2 * T), BF16), hg, NT)
    bias_tile = jnp.where(
        lax.broadcasted_iota(jnp.int32, (8, 128), 0) < 4, bias_rows[:, 0:128], bias_rows[:, 128:256]
    )
    bias_send[...] = bias_tile
    for device, k in near:
        send(bias_send, bias_buf.at[n], ss.at[9], rs.at[9], device)
    bias_buf[pl.ds(n, 1)] = bias_tile[None]
    act_full[...] = (pre * sigma).astype(BF16).reshape(COLS, W, 2 * T)
    for device, k in near:
        send(act_full.at[device[1]], act_buf.at[n], ss.at[4], rs.at[4], device)
    act_buf[pl.ds(n, 1)] = act_full[pl.ds(me, 1)]

    def total(buf, others, k):
        await_bytes(buf.at[pl.ds(0, others)], rs.at[k])
        return jnp.sum(buf[...].astype(F32), axis=0)

    def ring_sum():
        plane_sum = total(s1_buf, 31, 5)
        bias_sum = total(bias_buf, 7, 9)
        for h in range(2):
            ring_send[h] = jnp.concatenate(
                [plane_sum[8 * h : 8 * h + 8], bias_sum], axis=0
            ).astype(BF16)
        for d in offsets:
            device, half = along(d)
            send(ring_send.at[half], ring_buf.at[d + 8], ss.at[6], rs.at[6], device)
        ring_buf[pl.ds(8, 1)] = ring_send[pl.ds(zh, 1)]

    def backward(i, _):
        for u in range(0, UNROLL, 2):
            s = i * UNROLL + u
            p = two_products(
                ag_buf[rows_s[g, s]].reshape(W2, T),
                ag_buf[rows_s[g, s + 1]].reshape(W2, T),
                tvv[pl.ds(s, 2)],
            )
            prods[pl.ds(pl.multiple_of(s * W2, 2 * W2), 2 * W2), :] = p
        return 0

    await_bytes(ag_send.at[pl.ds(0, 7)], rs.at[3])
    own_ag.wait()
    turns = slots // UNROLL
    ring_sum()
    lax.fori_loop(0, turns, backward, 0)
    back = []
    for k, (peer, half) in enumerate(((prev, z_prev), (nxt, z_next))):
        select_sum(by_col[2 * k], prods, W2, half * W, W, TR, sums)
        halo_send[k] = sums[0 : TR * W, :].astype(BF16).reshape(TR, W, T)
        back.append(send(halo_send.at[k], halo_buf.at[k], back_ss.at[k], back_rs.at[k], peer))
    select_sum(by_col[1], prods, W2, zh * W, W, TR, sums)

    await_bytes(act_buf.at[pl.ds(0, 7)], rs.at[4])
    for k in range(8):
        act_o[:, k * 2 * T : (k + 1) * 2 * T] = act_buf[k]
    for copy in back:
        copy.wait_recv()
    for k in range(TR):
        fg_o[:, k * T : (k + 1) * T] = (
            sums[k * W : (k + 1) * W, :] + halo_buf[0, k].astype(F32) + halo_buf[1, k].astype(F32)
        ).astype(BF16)
    value = total(ring_buf, 15, 6).reshape(2, 8, T)
    y_send[...] = value
    for device in y_peers:
        send(y_send, y_buf.at[y], ss.at[8], rs.at[8], device)
    y_buf[pl.ds(y, 1)] = value[None]

    for copy in far_ft + [far_ct]:
        copy.wait_send()
    for k in range(4):
        await_bytes(win.at[0, 0], halo_ss.at[k])
    for copy in back:
        copy.wait_send()
    for k, view in (
        (0, cot_buf.at[pl.ds(0, 7)]),
        (1, cot_buf.at[pl.ds(0, 7)]),
        (2, agg_send.at[pl.ds(0, 7)]),
        (3, ag_send.at[pl.ds(0, 7)]),
        (4, act_buf.at[pl.ds(0, 7)]),
        (5, s1_buf.at[pl.ds(0, 31)]),
        (6, ring_buf.at[pl.ds(0, 15)]),
        (8, y_buf.at[pl.ds(0, 3)]),
        (9, bias_buf.at[pl.ds(0, 7)]),
    ):
        await_bytes(view, ss.at[k])
    await_bytes(y_buf.at[pl.ds(0, 3)], rs.at[8])
    for j in range(4):
        wg_o[(j // 2) * 8 : (j // 2 + 1) * 8, (j % 2) * T : (j % 2 + 1) * T] = y_buf[j, 0] * scale
    bias_sum = jnp.sum(y_buf[:, 1], axis=0)
    row = jnp.where(me < 8, bias_sum[0:1], bias_sum[4:5]) * scale
    bg_o[...] = pltpu.roll(row, (128 - (me % 8) * W) % 128, 1)[:, 0:W]


def on_device(features, tile_values, tile_rows, tile_cols, tile_count, weight, out_bias, cotangent):
    slots = tile_values.shape[1]
    nodes = features.shape[0]
    width = weight.shape[0]
    scale = 1.0 / math.sqrt(nodes * ROWS)
    vmem = pl.BlockSpec(memory_space=pltpu.VMEM)
    hbm = pl.BlockSpec(memory_space=pltpu.HBM)
    tiles = lambda *k: pltpu.VMEM(k + (8, T), F32)
    act, fg, wg, bg = pl.pallas_call(
        functools.partial(kernel, slots, scale),
        out_shape=(
            jax.ShapeDtypeStruct((W, nodes), BF16),
            jax.ShapeDtypeStruct((W, nodes), BF16),
            jax.ShapeDtypeStruct((W, width), F32),
            jax.ShapeDtypeStruct((1, W), F32),
        ),
        in_specs=[hbm] * 8,
        out_specs=(vmem,) * 4,
        scratch_shapes=[
            pltpu.SMEM(tile_rows.shape, jnp.int32),
            pltpu.SMEM(tile_cols.shape, jnp.int32),
            pltpu.SMEM(tile_count.shape, jnp.int32),
            pltpu.VMEM(tile_rows.shape, jnp.int32),
            pltpu.VMEM(tile_cols.shape, jnp.int32),
            pltpu.VMEM(weight.shape, BF16),
            pltpu.VMEM((1, width), F32),
            pltpu.VMEM((2, 3, W, nodes), BF16),
            pltpu.VMEM((3 * TR, W2, T), BF16),
            pltpu.VMEM((slots, T, T), BF16),
            pltpu.VMEM((slots, T, T), BF16),
            pltpu.VMEM((slots * W2, T), F32),
            pltpu.VMEM((TR * W2, T), F32),
            pltpu.VMEM((width, width), BF16),
            pltpu.VMEM((width, 2 * T), F32),
            pltpu.VMEM((W, nodes), BF16),
            pltpu.VMEM((COLS, W, 2 * T), BF16),
            pltpu.VMEM((8, 2, 2, W, T), BF16),
            pltpu.VMEM((4, 2, 2, 2, W, T), BF16),
            pltpu.VMEM((8, 2, 2, W, T), BF16),
            pltpu.VMEM((TR, 2, W, T), BF16),
            pltpu.VMEM((COLS, W, 2 * T), BF16),
            pltpu.VMEM((8, W, 2 * T), BF16),
            pltpu.VMEM((2, TR, W, T), BF16),
            pltpu.VMEM((2, TR, W, T), BF16),
            pltpu.VMEM((32, W, T), BF16),
            pltpu.VMEM((32, W, T), BF16),
            tiles(),
            tiles(8),
            pltpu.VMEM((2, W, T), BF16),
            pltpu.VMEM((16, W, T), BF16),
            tiles(2),
            tiles(4, 2),
            pltpu.SemaphoreType.DMA((CHUNKS,)),
            pltpu.SemaphoreType.DMA((9,)),
            pltpu.SemaphoreType.DMA((4,)),
            pltpu.SemaphoreType.DMA((4,)),
            pltpu.SemaphoreType.DMA((PIECES + 1,)),
            pltpu.SemaphoreType.DMA((PIECES + 1,)),
            pltpu.SemaphoreType.DMA((2,)),
            pltpu.SemaphoreType.DMA((2,)),
            pltpu.SemaphoreType.DMA((10,)),
            pltpu.SemaphoreType.DMA((10,)),
        ],
        compiler_params=pltpu.CompilerParams(
            collective_id=0, has_side_effects=True, vmem_limit_bytes=32 * 1024 * 1024
        ),
        name="graph_layer",
    )(
        features.T,
        cotangent.T,
        tile_values,
        tile_rows,
        tile_cols,
        tile_count,
        weight,
        out_bias.reshape(1, width),
    )
    return act.T, fg.T, wg, bg.reshape(W)


def solution(mesh):
    in_specs = (
        P("row", "col"),
        P("row", None, None, None),
        P(),
        P(),
        P(),
        P(),
        P(),
        P("row", "col"),
    )
    out_specs = (P("row", "col"), P("row", "col"), P("col", None), P("col"))
    return jax.shard_map(
        on_device, mesh=mesh, in_specs=in_specs, out_specs=out_specs, check_vma=False
    )
```

```python
import functools
import math

import jax
import jax.numpy as jnp
from jax import lax
from jax.experimental import pallas as pl
from jax.experimental.pallas import tpu as pltpu
from jax.sharding import PartitionSpec as P

MESH = pl.DeviceIdType.MESH
F32 = jnp.float32
BF16 = jnp.bfloat16
T = 128
TR = 16
W = 16
W2 = 2 * W
ROWS = 64
COLS = 16
UNROLL = 48
CHUNKS = 4
PIECES = 4
NT = (((1,), (1,)), ((), ()))
NN = (((1,), (0,)), ((), ()))


def dot(a, b, dims=NN):
    return lax.dot_general(a, b, dims, preferred_element_type=F32)


def select_sum(onehot, prods, stride, first, count, targets, out):
    slots = onehot.shape[1]
    for f in range(count):
        v = prods[pl.ds(first + f, slots, stride=stride), :]
        hi = v.astype(BF16)
        lo = (v - hi.astype(F32)).astype(BF16)
        out[pl.ds(f, targets, stride=count), :] = dot(onehot, hi) + dot(onehot, lo)


def two_products(first, second, tiles):
    none = jnp.zeros_like(first)
    both = jnp.concatenate(
        [jnp.concatenate([first, none], axis=1), jnp.concatenate([none, second], axis=1)], axis=0
    )
    return dot(both, tiles.reshape(2 * T, T))


def kernel(
    slots,
    scale,
    ft,
    ct,
    tv,
    rows_h,
    cols_h,
    count_h,
    w_h,
    bias_h,
    act_o,
    fg_o,
    wg_o,
    bg_o,
    rows_s,
    cols_s,
    count_s,
    rows_v,
    cols_v,
    w,
    bias,
    win,
    cols3,
    tvv,
    tvt,
    prods,
    sums,
    wt,
    bias_t,
    cot_far,
    cot_buf,
    agg_send,
    agg_buf,
    ag_send,
    ag_buf,
    act_full,
    act_buf,
    halo_send,
    halo_buf,
    s1_send,
    s1_buf,
    bias_send,
    bias_buf,
    ring_send,
    ring_buf,
    y_send,
    y_buf,
    tile_sem,
    own_sem,
    halo_ss,
    halo_rs,
    far_ss,
    far_rs,
    back_ss,
    back_rs,
    ss,
    rs,
):
    g = lax.axis_index("row")
    me = lax.axis_index("col")
    z_lo, y = g // 4, g % 4
    x, zh, core = me // 4, (me // 2) % 2, me % 2
    n = x * 2 + core
    other = (zh + 1) % 2
    mate = x * 4 + other * 2 + core
    z_prev, z_next = (zh + (ROWS - g) // ROWS) % 2, (zh + (g + 1) // ROWS) % 2
    prev = ((g + ROWS - 1) % ROWS, x * 4 + z_prev * 2 + core)
    nxt = ((g + 1) % ROWS, x * 4 + z_next * 2 + core)

    near = []
    plane = []
    for dx in (2, 1, 3, 0):
        for dy in (2, 1, 3, 0):
            for dc in (0, 1):
                px, py, pc = (x + dx) % 4, (y + dy) % 4, (core + dc) % 2
                if (dx, dy, dc) != (0, 0, 0):
                    device = (z_lo * 4 + py, px * 4 + zh * 2 + pc)
                    plane.append((device, (px * 2 + pc) * 4 + py))
                    if dy == 0:
                        near.append((device, px * 2 + pc))
    def along(offset):
        at = (zh * 16 + z_lo + offset + 32) % 32
        return ((at % 16) * 4 + y, x * 4 + (at // 16) * 2 + core), at // 16

    offsets = (-8, 7, -7, 6, -6, 5, -5, 4, -4, 3, -3, 2, -2, 1, -1)
    y_peers = [(z_lo * 4 + (y + d) % 4, me) for d in (1, 2, 3)]

    def wide(k):
        return pl.ds(pl.multiple_of(k * 2 * T, 2 * T), 2 * T)

    barrier = pltpu.get_barrier_semaphore()
    everyone = [(g, mate), prev, nxt]
    everyone += [along(-d)[0] for d in offsets]
    everyone += [device for device, _ in plane]
    for peer in everyone:
        pl.semaphore_signal(barrier, inc=1, device_id=peer, device_id_type=MESH)
    pl.semaphore_wait(barrier, len(everyone))

    def send(src, dst, send_sem, recv_sem, peer):
        copy = pltpu.make_async_remote_copy(
            src_ref=src,
            dst_ref=dst,
            send_sem=send_sem,
            recv_sem=recv_sem,
            device_id=peer,
            device_id_type=MESH,
        )
        copy.start()
        return copy

    def await_bytes(view, sem):
        pltpu.make_async_copy(view, view, sem).wait()

    cut = ft.shape[1] // PIECES
    pieces = [pl.ds(k * cut, cut) for k in range(PIECES)]
    far_ft = [
        send(ft.at[:, piece], win.at[zh, 1, :, piece], far_ss.at[k], far_rs.at[k], (g, mate))
        for k, piece in enumerate(pieces)
    ]

    step = slots // CHUNKS
    local = [
        pltpu.make_async_copy(src, dst, own_sem.at[k])
        for k, (src, dst) in enumerate(
            (
                (ft, win.at[zh, 1]),
                (ct.at[:, wide(n)], cot_buf.at[me]),
                (cols_h, cols_s),
                (rows_h, rows_s),
                (cols_h, cols_v),
                (rows_h, rows_v),
                (count_h, count_s),
                (w_h, w),
                (bias_h, bias),
            )
        )
    ] + [
        pltpu.make_async_copy(
            tv.at[0, pl.ds(k * step, step)], tvv.at[pl.ds(k * step, step)], tile_sem.at[k]
        )
        for k in range(CHUNKS)
    ]
    for copy in local:
        copy.start()

    def to_sides(src, half, piece):
        there = src.at[:, piece]
        send(there, win.at[half, 0, :, piece], halo_ss.at[half], halo_rs.at[half], nxt)
        send(there, win.at[half, 2, :, piece], halo_ss.at[2 + half], halo_rs.at[2 + half], prev)

    to_sides(ft, zh, pl.ds(0, ft.shape[1]))
    for device, k in near:
        send(ct.at[:, wide(k)], cot_buf.at[me], ss.at[0], rs.at[0], device)

    for copy in local:
        copy.wait()

    count = count_s[g]
    live = lax.broadcasted_iota(jnp.int32, (TR, slots), 1) < count
    row_ids = lax.broadcasted_iota(jnp.int32, (TR, slots), 0)
    by_row = jnp.where((rows_v[pl.ds(g, 1), :] == row_ids) & live, 1.0, 0.0).astype(BF16)
    own_cols = cols_v[pl.ds(g, 1), :]
    rel = ((lax.div(own_cols, TR) - g + (ROWS + 1)) % ROWS) * TR + lax.rem(own_cols, TR)
    by_col = [
        jnp.where((rel == row_ids + k * TR) & live, 1.0, 0.0).astype(BF16) for k in range(3)
    ]
    wt[...] = w[...].T
    bias_t[...] = jnp.broadcast_to(bias[...], (2 * T, W * COLS)).T

    def turn(i, _):
        for u in range(16):
            tvt[i * 16 + u] = tvv[i * 16 + u].T
        return 0

    lax.fori_loop(0, slots // 16, turn, 0)
    far_ct = send(ct, cot_far, far_ss.at[PIECES], far_rs.at[PIECES], (g, mate))
    for k, piece in enumerate(pieces):
        far_ft[k].wait_recv()
        to_sides(win.at[other, 1], other, piece)

    for k in range(4):
        await_bytes(win.at[0, 0], halo_rs.at[k])
    for h in range(2):
        for k in range(3):
            for b in range(TR):
                cols3[k * TR + b, h * W : (h + 1) * W] = win[h, k, :, b * T : (b + 1) * T]

    def columns_of(s):
        col = cols_s[g, s]
        grp = jnp.minimum(lax.rem(lax.div(col, TR) - g + (ROWS + 1), ROWS), 2)
        return cols3[grp * TR + lax.rem(col, TR)]

    def forward(i, _):
        for u in range(0, UNROLL, 2):
            s = i * UNROLL + u
            p = two_products(columns_of(s), columns_of(s + 1), tvt[pl.ds(s, 2)])
            prods[pl.ds(pl.multiple_of(s * W2, 2 * W2), 2 * W2), :] = p
        return 0

    lax.fori_loop(0, slots // UNROLL, forward, 0)
    def sum_rows(h):
        select_sum(by_row, prods, W2, h * W, W, TR, sums)
        for r in range(TR):
            agg_send[r // 2, h, r % 2] = sums[r * W : (r + 1) * W, :].astype(BF16)
        for device, k in near:
            send(agg_send.at[k, h], agg_buf.at[x, h, core], ss.at[2], rs.at[2], device)

    sum_rows(0)
    far_ct.wait_recv()
    own_cot = pltpu.make_async_copy(cot_far.at[:, wide(n)], cot_buf.at[mate], own_sem.at[1])
    own_cot.start()
    for device, k in near:
        send(cot_far.at[:, wide(k)], cot_buf.at[mate], ss.at[1], rs.at[1], device)
    sum_rows(1)
    own_agg = pltpu.make_async_copy(agg_send.at[n], agg_buf.at[x, :, core], own_sem.at[2])
    own_agg.start()
    await_bytes(cot_buf.at[pl.ds(0, 7)], rs.at[0])
    await_bytes(cot_buf.at[pl.ds(0, 7)], rs.at[1])
    own_cot.wait()
    own_agg.wait()
    await_bytes(agg_send.at[pl.ds(0, 7)], rs.at[2])

    agg_t = jnp.concatenate(
        [agg_buf[:, :, :, t].reshape(COLS * W, T) for t in range(2)], axis=1
    )
    pre = dot(wt[...], agg_t) + bias_t[...]
    sigma = jax.nn.sigmoid(pre)
    cot = cot_buf[...].reshape(COLS * W, 2 * T).astype(F32)
    hg = (cot * sigma * (1.0 + pre * (1.0 - sigma))).astype(BF16)
    ag = dot(w[...], hg).astype(BF16)
    for k in range(8):
        for h in range(2):
            first = ((k // 2) * 4 + h * 2 + k % 2) * W
            for t in range(2):
                ag_send[k, t, h] = ag[first : first + W, t * T : (t + 1) * T]
    for device, k in near:
        send(ag_send.at[k], ag_buf.at[pl.ds(2 * n, 2)], ss.at[3], rs.at[3], device)
    own_ag = pltpu.make_async_copy(ag_send.at[n], ag_buf.at[pl.ds(2 * n, 2)], own_sem.at[3])
    own_ag.start()

    wg = dot(agg_t, hg, NT)
    for k in range(8):
        for j in range(4):
            first = ((k // 2) * 4 + k % 2) * W + (j // 2) * 8
            across = slice((j % 2) * T, (j % 2 + 1) * T)
            s1_send[k * 4 + j] = jnp.concatenate(
                [wg[first : first + 8, across], wg[first + 2 * W : first + 2 * W + 8, across]], axis=0
            ).astype(BF16)
    for device, k in plane:
        send(s1_send.at[k], s1_buf.at[n * 4 + y], ss.at[5], rs.at[5], device)
    s1_buf[pl.ds(n * 4 + y, 1)] = s1_send[pl.ds(n * 4 + y, 1)]
    bias_rows = dot(jnp.ones((8, 2 * T), BF16), hg, NT)
    bias_tile = jnp.where(
        lax.broadcasted_iota(jnp.int32, (8, 128), 0) < 4, bias_rows[:, 0:128], bias_rows[:, 128:256]
    )
    bias_send[...] = bias_tile
    for device, k in near:
        send(bias_send, bias_buf.at[n], ss.at[9], rs.at[9], device)
    bias_buf[pl.ds(n, 1)] = bias_tile[None]
    act_full[...] = (pre * sigma).astype(BF16).reshape(COLS, W, 2 * T)

    def total(buf, others, k):
        await_bytes(buf.at[pl.ds(0, others)], rs.at[k])
        return jnp.sum(buf[...].astype(F32), axis=0)

    def ring_sum():
        plane_sum = total(s1_buf, 31, 5)
        bias_sum = total(bias_buf, 7, 9)
        for h in range(2):
            ring_send[h] = jnp.concatenate(
                [plane_sum[8 * h : 8 * h + 8], bias_sum], axis=0
            ).astype(BF16)
        for d in offsets:
            device, half = along(d)
            send(ring_send.at[half], ring_buf.at[d + 8], ss.at[6], rs.at[6], device)
        ring_buf[pl.ds(8, 1)] = ring_send[pl.ds(zh, 1)]

    def backward(i, _):
        for u in range(0, UNROLL, 2):
            s = i * UNROLL + u
            p = two_products(
                ag_buf[rows_s[g, s]].reshape(W2, T),
                ag_buf[rows_s[g, s + 1]].reshape(W2, T),
                tvv[pl.ds(s, 2)],
            )
            prods[pl.ds(pl.multiple_of(s * W2, 2 * W2), 2 * W2), :] = p
        return 0

    await_bytes(ag_send.at[pl.ds(0, 7)], rs.at[3])
    own_ag.wait()
    turns = slots // UNROLL
    ring_sum()
    lax.fori_loop(0, turns, backward, 0)
    back = []
    for k, (peer, half) in enumerate(((prev, z_prev), (nxt, z_next))):
        select_sum(by_col[2 * k], prods, W2, half * W, W, TR, sums)
        halo_send[k] = sums[0 : TR * W, :].astype(BF16).reshape(TR, W, T)
        back.append(send(halo_send.at[k], halo_buf.at[k], back_ss.at[k], back_rs.at[k], peer))
    for device, k in near:
        send(act_full.at[device[1]], act_buf.at[n], ss.at[4], rs.at[4], device)
    act_buf[pl.ds(n, 1)] = act_full[pl.ds(me, 1)]
    select_sum(by_col[1], prods, W2, zh * W, W, TR, sums)

    await_bytes(act_buf.at[pl.ds(0, 7)], rs.at[4])
    for k in range(8):
        act_o[:, k * 2 * T : (k + 1) * 2 * T] = act_buf[k]
    for copy in back:
        copy.wait_recv()
    for k in range(TR):
        fg_o[:, k * T : (k + 1) * T] = (
            sums[k * W : (k + 1) * W, :] + halo_buf[0, k].astype(F32) + halo_buf[1, k].astype(F32)
        ).astype(BF16)
    value = total(ring_buf, 15, 6).reshape(2, 8, T)
    y_send[...] = value
    for device in y_peers:
        send(y_send, y_buf.at[y], ss.at[8], rs.at[8], device)
    y_buf[pl.ds(y, 1)] = value[None]

    for copy in far_ft + [far_ct]:
        copy.wait_send()
    for k in range(4):
        await_bytes(win.at[0, 0], halo_ss.at[k])
    for copy in back:
        copy.wait_send()
    for k, view in (
        (0, cot_buf.at[pl.ds(0, 7)]),
        (1, cot_buf.at[pl.ds(0, 7)]),
        (2, agg_send.at[pl.ds(0, 7)]),
        (3, ag_send.at[pl.ds(0, 7)]),
        (4, act_buf.at[pl.ds(0, 7)]),
        (5, s1_buf.at[pl.ds(0, 31)]),
        (6, ring_buf.at[pl.ds(0, 15)]),
        (8, y_buf.at[pl.ds(0, 3)]),
        (9, bias_buf.at[pl.ds(0, 7)]),
    ):
        await_bytes(view, ss.at[k])
    await_bytes(y_buf.at[pl.ds(0, 3)], rs.at[8])
    for j in range(4):
        wg_o[(j // 2) * 8 : (j // 2 + 1) * 8, (j % 2) * T : (j % 2 + 1) * T] = y_buf[j, 0] * scale
    bias_sum = jnp.sum(y_buf[:, 1], axis=0)
    row = jnp.where(me < 8, bias_sum[0:1], bias_sum[4:5]) * scale
    bg_o[...] = pltpu.roll(row, (128 - (me % 8) * W) % 128, 1)[:, 0:W]


def on_device(features, tile_values, tile_rows, tile_cols, tile_count, weight, out_bias, cotangent):
    slots = tile_values.shape[1]
    nodes = features.shape[0]
    width = weight.shape[0]
    scale = 1.0 / math.sqrt(nodes * ROWS)
    vmem = pl.BlockSpec(memory_space=pltpu.VMEM)
    hbm = pl.BlockSpec(memory_space=pltpu.HBM)
    tiles = lambda *k: pltpu.VMEM(k + (8, T), F32)
    act, fg, wg, bg = pl.pallas_call(
        functools.partial(kernel, slots, scale),
        out_shape=(
            jax.ShapeDtypeStruct((W, nodes), BF16),
            jax.ShapeDtypeStruct((W, nodes), BF16),
            jax.ShapeDtypeStruct((W, width), F32),
            jax.ShapeDtypeStruct((1, W), F32),
        ),
        in_specs=[hbm] * 8,
        out_specs=(vmem,) * 4,
        scratch_shapes=[
            pltpu.SMEM(tile_rows.shape, jnp.int32),
            pltpu.SMEM(tile_cols.shape, jnp.int32),
            pltpu.SMEM(tile_count.shape, jnp.int32),
            pltpu.VMEM(tile_rows.shape, jnp.int32),
            pltpu.VMEM(tile_cols.shape, jnp.int32),
            pltpu.VMEM(weight.shape, BF16),
            pltpu.VMEM((1, width), F32),
            pltpu.VMEM((2, 3, W, nodes), BF16),
            pltpu.VMEM((3 * TR, W2, T), BF16),
            pltpu.VMEM((slots, T, T), BF16),
            pltpu.VMEM((slots, T, T), BF16),
            pltpu.VMEM((slots * W2, T), F32),
            pltpu.VMEM((TR * W2, T), F32),
            pltpu.VMEM((width, width), BF16),
            pltpu.VMEM((width, 2 * T), F32),
            pltpu.VMEM((W, nodes), BF16),
            pltpu.VMEM((COLS, W, 2 * T), BF16),
            pltpu.VMEM((8, 2, 2, W, T), BF16),
            pltpu.VMEM((4, 2, 2, 2, W, T), BF16),
            pltpu.VMEM((8, 2, 2, W, T), BF16),
            pltpu.VMEM((TR, 2, W, T), BF16),
            pltpu.VMEM((COLS, W, 2 * T), BF16),
            pltpu.VMEM((8, W, 2 * T), BF16),
            pltpu.VMEM((2, TR, W, T), BF16),
            pltpu.VMEM((2, TR, W, T), BF16),
            pltpu.VMEM((32, W, T), BF16),
            pltpu.VMEM((32, W, T), BF16),
            tiles(),
            tiles(8),
            pltpu.VMEM((2, W, T), BF16),
            pltpu.VMEM((16, W, T), BF16),
            tiles(2),
            tiles(4, 2),
            pltpu.SemaphoreType.DMA((CHUNKS,)),
            pltpu.SemaphoreType.DMA((9,)),
            pltpu.SemaphoreType.DMA((4,)),
            pltpu.SemaphoreType.DMA((4,)),
            pltpu.SemaphoreType.DMA((PIECES + 1,)),
            pltpu.SemaphoreType.DMA((PIECES + 1,)),
            pltpu.SemaphoreType.DMA((2,)),
            pltpu.SemaphoreType.DMA((2,)),
            pltpu.SemaphoreType.DMA((10,)),
            pltpu.SemaphoreType.DMA((10,)),
        ],
        compiler_params=pltpu.CompilerParams(
            collective_id=0, has_side_effects=True, vmem_limit_bytes=32 * 1024 * 1024
        ),
        name="graph_layer",
    )(
        features.T,
        cotangent.T,
        tile_values,
        tile_rows,
        tile_cols,
        tile_count,
        weight,
        out_bias.reshape(1, width),
    )
    return act.T, fg.T, wg, bg.reshape(W)


def solution(mesh):
    in_specs = (
        P("row", "col"),
        P("row", None, None, None),
        P(),
        P(),
        P(),
        P(),
        P(),
        P("row", "col"),
    )
    out_specs = (P("row", "col"), P("row", "col"), P("col", None), P("col"))
    return jax.shard_map(
        on_device, mesh=mesh, in_specs=in_specs, out_specs=out_specs, check_vma=False
    )
```

```python
import functools
import math

import jax
import jax.numpy as jnp
from jax import lax
from jax.experimental import pallas as pl
from jax.experimental.pallas import tpu as pltpu
from jax.sharding import PartitionSpec as P

MESH = pl.DeviceIdType.MESH
F32 = jnp.float32
BF16 = jnp.bfloat16
T = 128
TR = 16
W = 16
W2 = 2 * W
ROWS = 64
COLS = 16
UNROLL = 48
CHUNKS = 4
PIECES = 4
NT = (((1,), (1,)), ((), ()))
NN = (((1,), (0,)), ((), ()))


def dot(a, b, dims=NN):
    return lax.dot_general(a, b, dims, preferred_element_type=F32)


def select_sum(onehot, prods, stride, first, count, targets, out):
    slots = onehot.shape[1]
    for f in range(count):
        v = prods[pl.ds(first + f, slots, stride=stride), :]
        hi = v.astype(BF16)
        lo = (v - hi.astype(F32)).astype(BF16)
        out[pl.ds(f, targets, stride=count), :] = dot(onehot, hi) + dot(onehot, lo)


def two_products(first, second, tiles):
    none = jnp.zeros_like(first)
    both = jnp.concatenate(
        [jnp.concatenate([first, none], axis=1), jnp.concatenate([none, second], axis=1)], axis=0
    )
    return dot(both, tiles.reshape(2 * T, T))


def kernel(
    slots,
    scale,
    ft,
    ct,
    tv,
    rows_h,
    cols_h,
    count_h,
    w_h,
    bias_h,
    act_o,
    fg_o,
    wg_o,
    bg_o,
    rows_s,
    cols_s,
    count_s,
    rows_v,
    cols_v,
    w,
    bias,
    win,
    cols3,
    tvv,
    tvt,
    prods,
    sums,
    wt,
    bias_t,
    cot_far,
    cot_buf,
    agg_send,
    agg_buf,
    ag_send,
    ag_buf,
    act_full,
    act_buf,
    halo_send,
    halo_buf,
    s1_send,
    s1_buf,
    bias_send,
    bias_buf,
    ring_send,
    ring_buf,
    y_send,
    y_buf,
    tile_sem,
    own_sem,
    halo_ss,
    halo_rs,
    far_ss,
    far_rs,
    back_ss,
    back_rs,
    ss,
    rs,
):
    g = lax.axis_index("row")
    me = lax.axis_index("col")
    z_lo, y = g // 4, g % 4
    x, zh, core = me // 4, (me // 2) % 2, me % 2
    n = x * 2 + core
    other = (zh + 1) % 2
    mate = x * 4 + other * 2 + core
    z_prev, z_next = (zh + (ROWS - g) // ROWS) % 2, (zh + (g + 1) // ROWS) % 2
    prev = ((g + ROWS - 1) % ROWS, x * 4 + z_prev * 2 + core)
    nxt = ((g + 1) % ROWS, x * 4 + z_next * 2 + core)

    near = []
    plane = []
    for dx in (2, 1, 3, 0):
        for dy in (2, 1, 3, 0):
            for dc in (0, 1):
                px, py, pc = (x + dx) % 4, (y + dy) % 4, (core + dc) % 2
                if (dx, dy, dc) != (0, 0, 0):
                    device = (z_lo * 4 + py, px * 4 + zh * 2 + pc)
                    plane.append((device, (px * 2 + pc) * 4 + py))
                    if dy == 0:
                        near.append((device, px * 2 + pc))
    def along(offset):
        at = (zh * 16 + z_lo + offset + 32) % 32
        return ((at % 16) * 4 + y, x * 4 + (at // 16) * 2 + core), at // 16

    offsets = (-8, 7, -7, 6, -6, 5, -5, 4, -4, 3, -3, 2, -2, 1, -1)
    y_peers = [(z_lo * 4 + (y + d) % 4, me) for d in (1, 2, 3)]

    def wide(k):
        return pl.ds(pl.multiple_of(k * 2 * T, 2 * T), 2 * T)

    barrier = pltpu.get_barrier_semaphore()
    everyone = [(g, mate), prev, nxt]
    everyone += [along(-d)[0] for d in offsets]
    everyone += [device for device, _ in plane]
    for peer in everyone:
        pl.semaphore_signal(barrier, inc=1, device_id=peer, device_id_type=MESH)
    step = slots // CHUNKS
    local = [
        pltpu.make_async_copy(src, dst, own_sem.at[k])
        for k, (src, dst) in enumerate(
            (
                (ft, win.at[zh, 1]),
                (ct.at[:, wide(n)], cot_buf.at[me]),
                (cols_h, cols_s),
                (rows_h, rows_s),
                (cols_h, cols_v),
                (rows_h, rows_v),
                (count_h, count_s),
                (w_h, w),
                (bias_h, bias),
            )
        )
    ] + [
        pltpu.make_async_copy(
            tv.at[0, pl.ds(k * step, step)], tvv.at[pl.ds(k * step, step)], tile_sem.at[k]
        )
        for k in range(CHUNKS)
    ]
    for copy in local:
        copy.start()
    for copy in local:
        copy.wait()

    count = count_s[g]
    live = lax.broadcasted_iota(jnp.int32, (TR, slots), 1) < count
    row_ids = lax.broadcasted_iota(jnp.int32, (TR, slots), 0)
    by_row = jnp.where((rows_v[pl.ds(g, 1), :] == row_ids) & live, 1.0, 0.0).astype(BF16)
    own_cols = cols_v[pl.ds(g, 1), :]
    rel = ((lax.div(own_cols, TR) - g + (ROWS + 1)) % ROWS) * TR + lax.rem(own_cols, TR)
    by_col = [
        jnp.where((rel == row_ids + k * TR) & live, 1.0, 0.0).astype(BF16) for k in range(3)
    ]
    wt[...] = w[...].T
    bias_t[...] = jnp.broadcast_to(bias[...], (2 * T, W * COLS)).T

    def turn(i, _):
        for u in range(16):
            tvt[i * 16 + u] = tvv[i * 16 + u].T
        return 0

    lax.fori_loop(0, slots // 16, turn, 0)

    pl.semaphore_wait(barrier, len(everyone))

    def send(src, dst, send_sem, recv_sem, peer):
        copy = pltpu.make_async_remote_copy(
            src_ref=src,
            dst_ref=dst,
            send_sem=send_sem,
            recv_sem=recv_sem,
            device_id=peer,
            device_id_type=MESH,
        )
        copy.start()
        return copy

    def await_bytes(view, sem):
        pltpu.make_async_copy(view, view, sem).wait()

    cut = ft.shape[1] // PIECES
    pieces = [pl.ds(k * cut, cut) for k in range(PIECES)]
    far_ft = [
        send(ft.at[:, piece], win.at[zh, 1, :, piece], far_ss.at[k], far_rs.at[k], (g, mate))
        for k, piece in enumerate(pieces)
    ]

    def to_sides(src, half, piece):
        there = src.at[:, piece]
        send(there, win.at[half, 0, :, piece], halo_ss.at[half], halo_rs.at[half], nxt)
        send(there, win.at[half, 2, :, piece], halo_ss.at[2 + half], halo_rs.at[2 + half], prev)

    to_sides(ft, zh, pl.ds(0, ft.shape[1]))
    for device, k in near:
        send(ct.at[:, wide(k)], cot_buf.at[me], ss.at[0], rs.at[0], device)

    for copy in far_ft:
        copy.wait_send()
    far_ct = send(ct, cot_far, far_ss.at[PIECES], far_rs.at[PIECES], (g, mate))
    for k, piece in enumerate(pieces):
        far_ft[k].wait_recv()
        to_sides(win.at[other, 1], other, piece)

    for k in range(4):
        await_bytes(win.at[0, 0], halo_rs.at[k])
    for h in range(2):
        for k in range(3):
            for b in range(TR):
                cols3[k * TR + b, h * W : (h + 1) * W] = win[h, k, :, b * T : (b + 1) * T]

    def columns_of(s):
        col = cols_s[g, s]
        grp = jnp.minimum(lax.rem(lax.div(col, TR) - g + (ROWS + 1), ROWS), 2)
        return cols3[grp * TR + lax.rem(col, TR)]

    def forward(i, _):
        for u in range(0, UNROLL, 2):
            s = i * UNROLL + u
            p = two_products(columns_of(s), columns_of(s + 1), tvt[pl.ds(s, 2)])
            prods[pl.ds(pl.multiple_of(s * W2, 2 * W2), 2 * W2), :] = p
        return 0

    lax.fori_loop(0, slots // UNROLL, forward, 0)
    def sum_rows(h):
        select_sum(by_row, prods, W2, h * W, W, TR, sums)
        for r in range(TR):
            agg_send[r // 2, h, r % 2] = sums[r * W : (r + 1) * W, :].astype(BF16)
        for device, k in near:
            send(agg_send.at[k, h], agg_buf.at[x, h, core], ss.at[2], rs.at[2], device)

    sum_rows(0)
    far_ct.wait_recv()
    own_cot = pltpu.make_async_copy(cot_far.at[:, wide(n)], cot_buf.at[mate], own_sem.at[1])
    own_cot.start()
    for device, k in near:
        send(cot_far.at[:, wide(k)], cot_buf.at[mate], ss.at[1], rs.at[1], device)
    sum_rows(1)
    own_agg = pltpu.make_async_copy(agg_send.at[n], agg_buf.at[x, :, core], own_sem.at[2])
    own_agg.start()
    await_bytes(cot_buf.at[pl.ds(0, 7)], rs.at[0])
    await_bytes(cot_buf.at[pl.ds(0, 7)], rs.at[1])
    own_cot.wait()
    own_agg.wait()
    await_bytes(agg_send.at[pl.ds(0, 7)], rs.at[2])

    agg_t = jnp.concatenate(
        [agg_buf[:, :, :, t].reshape(COLS * W, T) for t in range(2)], axis=1
    )
    pre = dot(wt[...], agg_t) + bias_t[...]
    sigma = jax.nn.sigmoid(pre)
    cot = cot_buf[...].reshape(COLS * W, 2 * T).astype(F32)
    hg = (cot * sigma * (1.0 + pre * (1.0 - sigma))).astype(BF16)
    ag = dot(w[...], hg).astype(BF16)
    for k in range(8):
        for h in range(2):
            first = ((k // 2) * 4 + h * 2 + k % 2) * W
            for t in range(2):
                ag_send[k, t, h] = ag[first : first + W, t * T : (t + 1) * T]
    for device, k in near:
        send(ag_send.at[k], ag_buf.at[pl.ds(2 * n, 2)], ss.at[3], rs.at[3], device)
    own_ag = pltpu.make_async_copy(ag_send.at[n], ag_buf.at[pl.ds(2 * n, 2)], own_sem.at[3])
    own_ag.start()

    wg = dot(agg_t, hg, NT)
    for k in range(8):
        for j in range(4):
            first = ((k // 2) * 4 + k % 2) * W + (j // 2) * 8
            across = slice((j % 2) * T, (j % 2 + 1) * T)
            s1_send[k * 4 + j] = jnp.concatenate(
                [wg[first : first + 8, across], wg[first + 2 * W : first + 2 * W + 8, across]], axis=0
            ).astype(BF16)
    for device, k in plane:
        send(s1_send.at[k], s1_buf.at[n * 4 + y], ss.at[5], rs.at[5], device)
    s1_buf[pl.ds(n * 4 + y, 1)] = s1_send[pl.ds(n * 4 + y, 1)]
    bias_rows = dot(jnp.ones((8, 2 * T), BF16), hg, NT)
    bias_tile = jnp.where(
        lax.broadcasted_iota(jnp.int32, (8, 128), 0) < 4, bias_rows[:, 0:128], bias_rows[:, 128:256]
    )
    bias_send[...] = bias_tile
    for device, k in near:
        send(bias_send, bias_buf.at[n], ss.at[9], rs.at[9], device)
    bias_buf[pl.ds(n, 1)] = bias_tile[None]
    act_full[...] = (pre * sigma).astype(BF16).reshape(COLS, W, 2 * T)

    def total(buf, others, k):
        await_bytes(buf.at[pl.ds(0, others)], rs.at[k])
        return jnp.sum(buf[...].astype(F32), axis=0)

    def ring_sum():
        plane_sum = total(s1_buf, 31, 5)
        bias_sum = total(bias_buf, 7, 9)
        for h in range(2):
            ring_send[h] = jnp.concatenate(
                [plane_sum[8 * h : 8 * h + 8], bias_sum], axis=0
            ).astype(BF16)
        for d in offsets:
            device, half = along(d)
            send(ring_send.at[half], ring_buf.at[d + 8], ss.at[6], rs.at[6], device)
        ring_buf[pl.ds(8, 1)] = ring_send[pl.ds(zh, 1)]

    def backward(i, _):
        for u in range(0, UNROLL, 2):
            s = i * UNROLL + u
            p = two_products(
                ag_buf[rows_s[g, s]].reshape(W2, T),
                ag_buf[rows_s[g, s + 1]].reshape(W2, T),
                tvv[pl.ds(s, 2)],
            )
            prods[pl.ds(pl.multiple_of(s * W2, 2 * W2), 2 * W2), :] = p
        return 0

    await_bytes(ag_send.at[pl.ds(0, 7)], rs.at[3])
    own_ag.wait()
    turns = slots // UNROLL
    ring_sum()
    lax.fori_loop(0, turns, backward, 0)
    back = []
    for k, (peer, half) in enumerate(((prev, z_prev), (nxt, z_next))):
        select_sum(by_col[2 * k], prods, W2, half * W, W, TR, sums)
        halo_send[k] = sums[0 : TR * W, :].astype(BF16).reshape(TR, W, T)
        back.append(send(halo_send.at[k], halo_buf.at[k], back_ss.at[k], back_rs.at[k], peer))
    for device, k in near:
        send(act_full.at[device[1]], act_buf.at[n], ss.at[4], rs.at[4], device)
    act_buf[pl.ds(n, 1)] = act_full[pl.ds(me, 1)]
    select_sum(by_col[1], prods, W2, zh * W, W, TR, sums)

    await_bytes(act_buf.at[pl.ds(0, 7)], rs.at[4])
    for k in range(8):
        act_o[:, k * 2 * T : (k + 1) * 2 * T] = act_buf[k]
    for copy in back:
        copy.wait_recv()
    for k in range(TR):
        fg_o[:, k * T : (k + 1) * T] = (
            sums[k * W : (k + 1) * W, :] + halo_buf[0, k].astype(F32) + halo_buf[1, k].astype(F32)
        ).astype(BF16)
    value = total(ring_buf, 15, 6).reshape(2, 8, T)
    y_send[...] = value
    for device in y_peers:
        send(y_send, y_buf.at[y], ss.at[8], rs.at[8], device)
    y_buf[pl.ds(y, 1)] = value[None]

    far_ct.wait_send()
    for k in range(4):
        await_bytes(win.at[0, 0], halo_ss.at[k])
    for copy in back:
        copy.wait_send()
    for k, view in (
        (0, cot_buf.at[pl.ds(0, 7)]),
        (1, cot_buf.at[pl.ds(0, 7)]),
        (2, agg_send.at[pl.ds(0, 7)]),
        (3, ag_send.at[pl.ds(0, 7)]),
        (4, act_buf.at[pl.ds(0, 7)]),
        (5, s1_buf.at[pl.ds(0, 31)]),
        (6, ring_buf.at[pl.ds(0, 15)]),
        (8, y_buf.at[pl.ds(0, 3)]),
        (9, bias_buf.at[pl.ds(0, 7)]),
    ):
        await_bytes(view, ss.at[k])
    await_bytes(y_buf.at[pl.ds(0, 3)], rs.at[8])
    for j in range(4):
        wg_o[(j // 2) * 8 : (j // 2 + 1) * 8, (j % 2) * T : (j % 2 + 1) * T] = y_buf[j, 0] * scale
    bias_sum = jnp.sum(y_buf[:, 1], axis=0)
    row = jnp.where(me < 8, bias_sum[0:1], bias_sum[4:5]) * scale
    bg_o[...] = pltpu.roll(row, (128 - (me % 8) * W) % 128, 1)[:, 0:W]


def on_device(features, tile_values, tile_rows, tile_cols, tile_count, weight, out_bias, cotangent):
    slots = tile_values.shape[1]
    nodes = features.shape[0]
    width = weight.shape[0]
    scale = 1.0 / math.sqrt(nodes * ROWS)
    vmem = pl.BlockSpec(memory_space=pltpu.VMEM)
    hbm = pl.BlockSpec(memory_space=pltpu.HBM)
    tiles = lambda *k: pltpu.VMEM(k + (8, T), F32)
    act, fg, wg, bg = pl.pallas_call(
        functools.partial(kernel, slots, scale),
        out_shape=(
            jax.ShapeDtypeStruct((W, nodes), BF16),
            jax.ShapeDtypeStruct((W, nodes), BF16),
            jax.ShapeDtypeStruct((W, width), F32),
            jax.ShapeDtypeStruct((1, W), F32),
        ),
        in_specs=[hbm] * 8,
        out_specs=(vmem,) * 4,
        scratch_shapes=[
            pltpu.SMEM(tile_rows.shape, jnp.int32),
            pltpu.SMEM(tile_cols.shape, jnp.int32),
            pltpu.SMEM(tile_count.shape, jnp.int32),
            pltpu.VMEM(tile_rows.shape, jnp.int32),
            pltpu.VMEM(tile_cols.shape, jnp.int32),
            pltpu.VMEM(weight.shape, BF16),
            pltpu.VMEM((1, width), F32),
            pltpu.VMEM((2, 3, W, nodes), BF16),
            pltpu.VMEM((3 * TR, W2, T), BF16),
            pltpu.VMEM((slots, T, T), BF16),
            pltpu.VMEM((slots, T, T), BF16),
            pltpu.VMEM((slots * W2, T), F32),
            pltpu.VMEM((TR * W2, T), F32),
            pltpu.VMEM((width, width), BF16),
            pltpu.VMEM((width, 2 * T), F32),
            pltpu.VMEM((W, nodes), BF16),
            pltpu.VMEM((COLS, W, 2 * T), BF16),
            pltpu.VMEM((8, 2, 2, W, T), BF16),
            pltpu.VMEM((4, 2, 2, 2, W, T), BF16),
            pltpu.VMEM((8, 2, 2, W, T), BF16),
            pltpu.VMEM((TR, 2, W, T), BF16),
            pltpu.VMEM((COLS, W, 2 * T), BF16),
            pltpu.VMEM((8, W, 2 * T), BF16),
            pltpu.VMEM((2, TR, W, T), BF16),
            pltpu.VMEM((2, TR, W, T), BF16),
            pltpu.VMEM((32, W, T), BF16),
            pltpu.VMEM((32, W, T), BF16),
            tiles(),
            tiles(8),
            pltpu.VMEM((2, W, T), BF16),
            pltpu.VMEM((16, W, T), BF16),
            tiles(2),
            tiles(4, 2),
            pltpu.SemaphoreType.DMA((CHUNKS,)),
            pltpu.SemaphoreType.DMA((9,)),
            pltpu.SemaphoreType.DMA((4,)),
            pltpu.SemaphoreType.DMA((4,)),
            pltpu.SemaphoreType.DMA((PIECES + 1,)),
            pltpu.SemaphoreType.DMA((PIECES + 1,)),
            pltpu.SemaphoreType.DMA((2,)),
            pltpu.SemaphoreType.DMA((2,)),
            pltpu.SemaphoreType.DMA((10,)),
            pltpu.SemaphoreType.DMA((10,)),
        ],
        compiler_params=pltpu.CompilerParams(
            collective_id=0, has_side_effects=True, vmem_limit_bytes=32 * 1024 * 1024
        ),
        name="graph_layer",
    )(
        features.T,
        cotangent.T,
        tile_values,
        tile_rows,
        tile_cols,
        tile_count,
        weight,
        out_bias.reshape(1, width),
    )
    return act.T, fg.T, wg, bg.reshape(W)


def solution(mesh):
    in_specs = (
        P("row", "col"),
        P("row", None, None, None),
        P(),
        P(),
        P(),
        P(),
        P(),
        P("row", "col"),
    )
    out_specs = (P("row", "col"), P("row", "col"), P("col", None), P("col"))
    return jax.shard_map(
        on_device, mesh=mesh, in_specs=in_specs, out_specs=out_specs, check_vma=False
    )
```

```python
import functools
import math

import jax
import jax.numpy as jnp
from jax import lax
from jax.experimental import pallas as pl
from jax.experimental.pallas import tpu as pltpu
from jax.sharding import PartitionSpec as P

MESH = pl.DeviceIdType.MESH
F32 = jnp.float32
BF16 = jnp.bfloat16
T = 128
TR = 16
W = 16
W2 = 2 * W
ROWS = 64
COLS = 16
UNROLL = 48
CHUNKS = 4
PIECES = 4
NT = (((1,), (1,)), ((), ()))
NN = (((1,), (0,)), ((), ()))


def dot(a, b, dims=NN):
    return lax.dot_general(a, b, dims, preferred_element_type=F32)


def select_sum(onehot, prods, stride, first, count, targets, out):
    slots = onehot.shape[1]
    for f in range(count):
        v = prods[pl.ds(first + f, slots, stride=stride), :]
        hi = v.astype(BF16)
        lo = (v - hi.astype(F32)).astype(BF16)
        out[pl.ds(f, targets, stride=count), :] = dot(onehot, hi) + dot(onehot, lo)


def two_products(first, second, tiles):
    none = jnp.zeros_like(first)
    both = jnp.concatenate(
        [jnp.concatenate([first, none], axis=1), jnp.concatenate([none, second], axis=1)], axis=0
    )
    return dot(both, tiles.reshape(2 * T, T))


def kernel(
    slots,
    scale,
    ft,
    ct,
    tv,
    rows_h,
    cols_h,
    count_h,
    w_h,
    bias_h,
    act_o,
    fg_o,
    wg_o,
    bg_o,
    rows_s,
    cols_s,
    count_s,
    rows_v,
    cols_v,
    w,
    bias,
    win,
    cols3,
    tvv,
    tvt,
    prods,
    sums,
    wt,
    bias_t,
    cot_far,
    cot_buf,
    agg_send,
    agg_buf,
    ag_send,
    ag_buf,
    act_full,
    act_buf,
    halo_send,
    halo_buf,
    s1_send,
    s1_buf,
    bias_send,
    bias_buf,
    ring_send,
    ring_buf,
    y_send,
    y_buf,
    tile_sem,
    own_sem,
    halo_ss,
    halo_rs,
    far_ss,
    far_rs,
    back_ss,
    back_rs,
    ss,
    rs,
):
    g = lax.axis_index("row")
    me = lax.axis_index("col")
    z_lo, y = g // 4, g % 4
    x, zh, core = me // 4, (me // 2) % 2, me % 2
    n = x * 2 + core
    other = (zh + 1) % 2
    mate = x * 4 + other * 2 + core
    z_prev, z_next = (zh + (ROWS - g) // ROWS) % 2, (zh + (g + 1) // ROWS) % 2
    prev = ((g + ROWS - 1) % ROWS, x * 4 + z_prev * 2 + core)
    nxt = ((g + 1) % ROWS, x * 4 + z_next * 2 + core)

    near = []
    plane = []
    for dx in (2, 1, 3, 0):
        for dy in (2, 1, 3, 0):
            for dc in (0, 1):
                px, py, pc = (x + dx) % 4, (y + dy) % 4, (core + dc) % 2
                if (dx, dy, dc) != (0, 0, 0):
                    device = (z_lo * 4 + py, px * 4 + zh * 2 + pc)
                    plane.append((device, (px * 2 + pc) * 4 + py))
                    if dy == 0:
                        near.append((device, px * 2 + pc))
    def along(offset):
        at = (zh * 16 + z_lo + offset + 32) % 32
        return ((at % 16) * 4 + y, x * 4 + (at // 16) * 2 + core), at // 16

    offsets = (-8, 7, -7, 6, -6, 5, -5, 4, -4, 3, -3, 2, -2, 1, -1)
    y_peers = [(z_lo * 4 + (y + d) % 4, me) for d in (1, 2, 3)]

    def wide(k):
        return pl.ds(pl.multiple_of(k * 2 * T, 2 * T), 2 * T)

    barrier = pltpu.get_barrier_semaphore()
    everyone = [(g, mate), prev, nxt]
    everyone += [along(-d)[0] for d in offsets]
    everyone += [device for device, _ in plane]
    for peer in everyone:
        pl.semaphore_signal(barrier, inc=1, device_id=peer, device_id_type=MESH)
    pl.semaphore_wait(barrier, len(everyone))

    def send(src, dst, send_sem, recv_sem, peer):
        copy = pltpu.make_async_remote_copy(
            src_ref=src,
            dst_ref=dst,
            send_sem=send_sem,
            recv_sem=recv_sem,
            device_id=peer,
            device_id_type=MESH,
        )
        copy.start()
        return copy

    def await_bytes(view, sem):
        pltpu.make_async_copy(view, view, sem).wait()

    cut = ft.shape[1] // PIECES
    pieces = [pl.ds(k * cut, cut) for k in range(PIECES)]
    far_ft = [
        send(ft.at[:, piece], win.at[zh, 1, :, piece], far_ss.at[k], far_rs.at[k], (g, mate))
        for k, piece in enumerate(pieces)
    ]

    step = slots // CHUNKS
    local = [
        pltpu.make_async_copy(src, dst, own_sem.at[k])
        for k, (src, dst) in enumerate(
            (
                (ft, win.at[zh, 1]),
                (ct.at[:, wide(n)], cot_buf.at[me]),
                (cols_h, cols_s),
                (rows_h, rows_s),
                (cols_h, cols_v),
                (rows_h, rows_v),
                (count_h, count_s),
                (w_h, w),
                (bias_h, bias),
            )
        )
    ] + [
        pltpu.make_async_copy(
            tv.at[0, pl.ds(k * step, step)], tvv.at[pl.ds(k * step, step)], tile_sem.at[k]
        )
        for k in range(CHUNKS)
    ]
    for copy in local:
        copy.start()

    def to_sides(src, half, piece):
        there = src.at[:, piece]
        send(there, win.at[half, 0, :, piece], halo_ss.at[half], halo_rs.at[half], nxt)
        send(there, win.at[half, 2, :, piece], halo_ss.at[2 + half], halo_rs.at[2 + half], prev)

    to_sides(ft, zh, pl.ds(0, ft.shape[1]))
    for device, k in near:
        send(ct.at[:, wide(k)], cot_buf.at[me], ss.at[0], rs.at[0], device)

    for copy in far_ft:
        copy.wait_send()
    far_ct = send(ct, cot_far, far_ss.at[PIECES], far_rs.at[PIECES], (g, mate))

    for copy in local:
        copy.wait()

    count = count_s[g]
    live = lax.broadcasted_iota(jnp.int32, (TR, slots), 1) < count
    row_ids = lax.broadcasted_iota(jnp.int32, (TR, slots), 0)
    by_row = jnp.where((rows_v[pl.ds(g, 1), :] == row_ids) & live, 1.0, 0.0).astype(BF16)
    own_cols = cols_v[pl.ds(g, 1), :]
    rel = ((lax.div(own_cols, TR) - g + (ROWS + 1)) % ROWS) * TR + lax.rem(own_cols, TR)
    by_col = [
        jnp.where((rel == row_ids + k * TR) & live, 1.0, 0.0).astype(BF16) for k in range(3)
    ]
    wt[...] = w[...].T
    bias_t[...] = jnp.broadcast_to(bias[...], (2 * T, W * COLS)).T

    def turn(i, _):
        for u in range(16):
            tvt[i * 16 + u] = tvv[i * 16 + u].T
        return 0

    lax.fori_loop(0, slots // 16, turn, 0)
    for k, piece in enumerate(pieces):
        far_ft[k].wait_recv()
        to_sides(win.at[other, 1], other, piece)

    for k in range(4):
        await_bytes(win.at[0, 0], halo_rs.at[k])
    for h in range(2):
        for k in range(3):
            for b in range(TR):
                cols3[k * TR + b, h * W : (h + 1) * W] = win[h, k, :, b * T : (b + 1) * T]

    def columns_of(s):
        col = cols_s[g, s]
        grp = jnp.minimum(lax.rem(lax.div(col, TR) - g + (ROWS + 1), ROWS), 2)
        return cols3[grp * TR + lax.rem(col, TR)]

    def forward(i, _):
        for u in range(0, UNROLL, 2):
            s = i * UNROLL + u
            p = two_products(columns_of(s), columns_of(s + 1), tvt[pl.ds(s, 2)])
            prods[pl.ds(pl.multiple_of(s * W2, 2 * W2), 2 * W2), :] = p
        return 0

    lax.fori_loop(0, slots // UNROLL, forward, 0)
    def sum_rows(h):
        select_sum(by_row, prods, W2, h * W, W, TR, sums)
        for r in range(TR):
            agg_send[r // 2, h, r % 2] = sums[r * W : (r + 1) * W, :].astype(BF16)
        for device, k in near:
            send(agg_send.at[k, h], agg_buf.at[x, h, core], ss.at[2], rs.at[2], device)

    sum_rows(0)
    far_ct.wait_recv()
    own_cot = pltpu.make_async_copy(cot_far.at[:, wide(n)], cot_buf.at[mate], own_sem.at[1])
    own_cot.start()
    for device, k in near:
        send(cot_far.at[:, wide(k)], cot_buf.at[mate], ss.at[1], rs.at[1], device)
    sum_rows(1)
    own_agg = pltpu.make_async_copy(agg_send.at[n], agg_buf.at[x, :, core], own_sem.at[2])
    own_agg.start()
    await_bytes(cot_buf.at[pl.ds(0, 7)], rs.at[0])
    await_bytes(cot_buf.at[pl.ds(0, 7)], rs.at[1])
    own_cot.wait()
    own_agg.wait()
    await_bytes(agg_send.at[pl.ds(0, 7)], rs.at[2])

    agg_t = jnp.concatenate(
        [agg_buf[:, :, :, t].reshape(COLS * W, T) for t in range(2)], axis=1
    )
    pre = dot(wt[...], agg_t) + bias_t[...]
    sigma = jax.nn.sigmoid(pre)
    cot = cot_buf[...].reshape(COLS * W, 2 * T).astype(F32)
    hg = (cot * sigma * (1.0 + pre * (1.0 - sigma))).astype(BF16)
    ag = dot(w[...], hg).astype(BF16)
    for k in range(8):
        for h in range(2):
            first = ((k // 2) * 4 + h * 2 + k % 2) * W
            for t in range(2):
                ag_send[k, t, h] = ag[first : first + W, t * T : (t + 1) * T]
    for device, k in near:
        send(ag_send.at[k], ag_buf.at[pl.ds(2 * n, 2)], ss.at[3], rs.at[3], device)
    own_ag = pltpu.make_async_copy(ag_send.at[n], ag_buf.at[pl.ds(2 * n, 2)], own_sem.at[3])
    own_ag.start()

    wg = dot(agg_t, hg, NT)
    for k in range(8):
        for j in range(4):
            first = ((k // 2) * 4 + k % 2) * W + (j // 2) * 8
            across = slice((j % 2) * T, (j % 2 + 1) * T)
            s1_send[k * 4 + j] = jnp.concatenate(
                [wg[first : first + 8, across], wg[first + 2 * W : first + 2 * W + 8, across]], axis=0
            ).astype(BF16)
    for device, k in plane:
        send(s1_send.at[k], s1_buf.at[n * 4 + y], ss.at[5], rs.at[5], device)
    s1_buf[pl.ds(n * 4 + y, 1)] = s1_send[pl.ds(n * 4 + y, 1)]
    bias_rows = dot(jnp.ones((8, 2 * T), BF16), hg, NT)
    bias_tile = jnp.where(
        lax.broadcasted_iota(jnp.int32, (8, 128), 0) < 4, bias_rows[:, 0:128], bias_rows[:, 128:256]
    )
    bias_send[...] = bias_tile
    for device, k in near:
        send(bias_send, bias_buf.at[n], ss.at[9], rs.at[9], device)
    bias_buf[pl.ds(n, 1)] = bias_tile[None]
    act_full[...] = (pre * sigma).astype(BF16).reshape(COLS, W, 2 * T)

    def total(buf, others, k):
        await_bytes(buf.at[pl.ds(0, others)], rs.at[k])
        return jnp.sum(buf[...].astype(F32), axis=0)

    def ring_sum():
        plane_sum = total(s1_buf, 31, 5)
        bias_sum = total(bias_buf, 7, 9)
        for h in range(2):
            ring_send[h] = jnp.concatenate(
                [plane_sum[8 * h : 8 * h + 8], bias_sum], axis=0
            ).astype(BF16)
        for d in offsets:
            device, half = along(d)
            send(ring_send.at[half], ring_buf.at[d + 8], ss.at[6], rs.at[6], device)
        ring_buf[pl.ds(8, 1)] = ring_send[pl.ds(zh, 1)]

    def backward(i, _):
        for u in range(0, UNROLL, 2):
            s = i * UNROLL + u
            p = two_products(
                ag_buf[rows_s[g, s]].reshape(W2, T),
                ag_buf[rows_s[g, s + 1]].reshape(W2, T),
                tvv[pl.ds(s, 2)],
            )
            prods[pl.ds(pl.multiple_of(s * W2, 2 * W2), 2 * W2), :] = p
        return 0

    await_bytes(ag_send.at[pl.ds(0, 7)], rs.at[3])
    own_ag.wait()
    turns = slots // UNROLL
    ring_sum()
    lax.fori_loop(0, turns, backward, 0)
    back = []
    for k, (peer, half) in enumerate(((prev, z_prev), (nxt, z_next))):
        select_sum(by_col[2 * k], prods, W2, half * W, W, TR, sums)
        halo_send[k] = sums[0 : TR * W, :].astype(BF16).reshape(TR, W, T)
        back.append(send(halo_send.at[k], halo_buf.at[k], back_ss.at[k], back_rs.at[k], peer))
    for device, k in near:
        send(act_full.at[device[1]], act_buf.at[n], ss.at[4], rs.at[4], device)
    act_buf[pl.ds(n, 1)] = act_full[pl.ds(me, 1)]
    select_sum(by_col[1], prods, W2, zh * W, W, TR, sums)

    await_bytes(act_buf.at[pl.ds(0, 7)], rs.at[4])
    for k in range(8):
        act_o[:, k * 2 * T : (k + 1) * 2 * T] = act_buf[k]
    for copy in back:
        copy.wait_recv()
    for k in range(TR):
        fg_o[:, k * T : (k + 1) * T] = (
            sums[k * W : (k + 1) * W, :] + halo_buf[0, k].astype(F32) + halo_buf[1, k].astype(F32)
        ).astype(BF16)
    value = total(ring_buf, 15, 6).reshape(2, 8, T)
    y_send[...] = value
    for device in y_peers:
        send(y_send, y_buf.at[y], ss.at[8], rs.at[8], device)
    y_buf[pl.ds(y, 1)] = value[None]

    far_ct.wait_send()
    for k in range(4):
        await_bytes(win.at[0, 0], halo_ss.at[k])
    for copy in back:
        copy.wait_send()
    for k, view in (
        (0, cot_buf.at[pl.ds(0, 7)]),
        (1, cot_buf.at[pl.ds(0, 7)]),
        (2, agg_send.at[pl.ds(0, 7)]),
        (3, ag_send.at[pl.ds(0, 7)]),
        (4, act_buf.at[pl.ds(0, 7)]),
        (5, s1_buf.at[pl.ds(0, 31)]),
        (6, ring_buf.at[pl.ds(0, 15)]),
        (8, y_buf.at[pl.ds(0, 3)]),
        (9, bias_buf.at[pl.ds(0, 7)]),
    ):
        await_bytes(view, ss.at[k])
    await_bytes(y_buf.at[pl.ds(0, 3)], rs.at[8])
    for j in range(4):
        wg_o[(j // 2) * 8 : (j // 2 + 1) * 8, (j % 2) * T : (j % 2 + 1) * T] = y_buf[j, 0] * scale
    bias_sum = jnp.sum(y_buf[:, 1], axis=0)
    row = jnp.where(me < 8, bias_sum[0:1], bias_sum[4:5]) * scale
    bg_o[...] = pltpu.roll(row, (128 - (me % 8) * W) % 128, 1)[:, 0:W]


def on_device(features, tile_values, tile_rows, tile_cols, tile_count, weight, out_bias, cotangent):
    slots = tile_values.shape[1]
    nodes = features.shape[0]
    width = weight.shape[0]
    scale = 1.0 / math.sqrt(nodes * ROWS)
    vmem = pl.BlockSpec(memory_space=pltpu.VMEM)
    hbm = pl.BlockSpec(memory_space=pltpu.HBM)
    tiles = lambda *k: pltpu.VMEM(k + (8, T), F32)
    act, fg, wg, bg = pl.pallas_call(
        functools.partial(kernel, slots, scale),
        out_shape=(
            jax.ShapeDtypeStruct((W, nodes), BF16),
            jax.ShapeDtypeStruct((W, nodes), BF16),
            jax.ShapeDtypeStruct((W, width), F32),
            jax.ShapeDtypeStruct((1, W), F32),
        ),
        in_specs=[hbm] * 8,
        out_specs=(vmem,) * 4,
        scratch_shapes=[
            pltpu.SMEM(tile_rows.shape, jnp.int32),
            pltpu.SMEM(tile_cols.shape, jnp.int32),
            pltpu.SMEM(tile_count.shape, jnp.int32),
            pltpu.VMEM(tile_rows.shape, jnp.int32),
            pltpu.VMEM(tile_cols.shape, jnp.int32),
            pltpu.VMEM(weight.shape, BF16),
            pltpu.VMEM((1, width), F32),
            pltpu.VMEM((2, 3, W, nodes), BF16),
            pltpu.VMEM((3 * TR, W2, T), BF16),
            pltpu.VMEM((slots, T, T), BF16),
            pltpu.VMEM((slots, T, T), BF16),
            pltpu.VMEM((slots * W2, T), F32),
            pltpu.VMEM((TR * W2, T), F32),
            pltpu.VMEM((width, width), BF16),
            pltpu.VMEM((width, 2 * T), F32),
            pltpu.VMEM((W, nodes), BF16),
            pltpu.VMEM((COLS, W, 2 * T), BF16),
            pltpu.VMEM((8, 2, 2, W, T), BF16),
            pltpu.VMEM((4, 2, 2, 2, W, T), BF16),
            pltpu.VMEM((8, 2, 2, W, T), BF16),
            pltpu.VMEM((TR, 2, W, T), BF16),
            pltpu.VMEM((COLS, W, 2 * T), BF16),
            pltpu.VMEM((8, W, 2 * T), BF16),
            pltpu.VMEM((2, TR, W, T), BF16),
            pltpu.VMEM((2, TR, W, T), BF16),
            pltpu.VMEM((32, W, T), BF16),
            pltpu.VMEM((32, W, T), BF16),
            tiles(),
            tiles(8),
            pltpu.VMEM((2, W, T), BF16),
            pltpu.VMEM((16, W, T), BF16),
            tiles(2),
            tiles(4, 2),
            pltpu.SemaphoreType.DMA((CHUNKS,)),
            pltpu.SemaphoreType.DMA((9,)),
            pltpu.SemaphoreType.DMA((4,)),
            pltpu.SemaphoreType.DMA((4,)),
            pltpu.SemaphoreType.DMA((PIECES + 1,)),
            pltpu.SemaphoreType.DMA((PIECES + 1,)),
            pltpu.SemaphoreType.DMA((2,)),
            pltpu.SemaphoreType.DMA((2,)),
            pltpu.SemaphoreType.DMA((10,)),
            pltpu.SemaphoreType.DMA((10,)),
        ],
        compiler_params=pltpu.CompilerParams(
            collective_id=0, has_side_effects=True, vmem_limit_bytes=32 * 1024 * 1024
        ),
        name="graph_layer",
    )(
        features.T,
        cotangent.T,
        tile_values,
        tile_rows,
        tile_cols,
        tile_count,
        weight,
        out_bias.reshape(1, width),
    )
    return act.T, fg.T, wg, bg.reshape(W)


def solution(mesh):
    in_specs = (
        P("row", "col"),
        P("row", None, None, None),
        P(),
        P(),
        P(),
        P(),
        P(),
        P("row", "col"),
    )
    out_specs = (P("row", "col"), P("row", "col"), P("col", None), P("col"))
    return jax.shard_map(
        on_device, mesh=mesh, in_specs=in_specs, out_specs=out_specs, check_vma=False
    )
```
